32 devices in a mesh: lat: 4 (over x, core), lon: 8 (over z, y).
Axes of the slice: x: 2, y: 2, z: 4, core: 2. Of those that a mesh axis runs over, the one named last changes fastest.
Arguments:
- features: bfloat16 [16, 256, 256], P('lat', 'lon'), may hold values from -6 to 6
- cotangent: bfloat16 [16, 256, 256], P('lat', 'lon'), may hold values from -6 to 6
- weight: bfloat16 [4, 256, 256], replicated, may hold values from -0.1875 to 0.1875
- filter_taps: bfloat16 [16, 4, 5, 64], P('lat'), may hold values from -6 to 6
- lat_ext: int32 [16], P('lat'), may hold values from 1 to 3, as said below
- lon_count: int32 [16], P('lat'), may hold values from 1 to 32, as said below
Outputs:
- output: bfloat16 [16, 256, 256], P('lat', 'lon')
- field_grad: bfloat16 [16, 256, 256], P('lat', 'lon')
- weight_grad: float32 [4, 256, 256], replicated
The draws below stay inside these ranges and needn't reach their ends.
Inputs may be any that keep to these rules, and one draw needn't show every extreme that they name: `lat_ext`: a row uses the latitude offsets whose magnitude is below its entry. `lon_count`: a row uses the longitude offsets whose magnitude is below its entry.
All inputs are finite; a program needn't handle non-finite values.
Results may differ from the reference program's by a relative error of at most 0.006.
Values may be sent and summed in bfloat16 or wider, within the bound.
No kernel may reach another device: no remote copies, remote signals or barrier semaphores. Data moves between devices by JAX's collectives and lax.ppermute only.
A program may use at most 64 MiB of HBM per device.

```python
import math
import jax
import jax.numpy as jnp
from jax import lax

C = 256
K = 4
HLAT = 2
LON_DEV = 32
NDL = 5
NLAT = 16
NLON = 256


def draw_lat_ext(key, part):
    base_ext = jax.random.randint(key, (NLAT,), 1, HLAT + 2)
    full_row = jax.random.randint(jax.random.fold_in(key, 7), (), 0, NLAT)
    return jnp.where(jnp.arange(NLAT) == full_row, HLAT + 1, base_ext).astype(jnp.int32)


def draw_lon_count(key, part):
    row_ids = jnp.arange(NLAT, dtype=jnp.int32)
    distance = jnp.abs(2 * row_ids - (NLAT - 1))
    base_count = 1 + (LON_DEV - 1) * distance * distance // ((NLAT - 1) * (NLAT - 1))
    jitter = jax.random.randint(key, (NLAT,), 0, max(LON_DEV // 4, 2))
    return jnp.minimum(base_count + jitter, LON_DEV).astype(jnp.int32)


def levels(own_key, shape, split, least, largest):
    loudness = 1.0
    for dim, parts in split:
        steps = jax.random.uniform(jax.random.fold_in(jax.random.fold_in(own_key, 6), dim), (parts,), jnp.float32, least / len(split), largest / len(split))
        loudness = loudness * jnp.repeat(jnp.exp(steps), shape[dim] // parts).reshape((-1,) + (1,) * (len(shape) - 1 - dim))
    return loudness


def gaussian(stream_key, extent, deviation, limit, shards=(), kind=jnp.bfloat16):
    entries = deviation * jax.random.normal(stream_key, extent, jnp.float32)
    if shards:
        entries = entries * levels(stream_key, extent, shards, -0.22, 0.18)
    return jnp.clip(entries, -limit, limit).astype(kind)


def setup_inputs(seed: int = 0) -> dict:
    key_list = jax.random.split(jax.random.key(seed), 7)
    features = gaussian(key_list[0], (NLAT, NLON, C), 1.0, 6.0, ((0, 4), (1, 8)))
    cotangent = gaussian(key_list[1], (NLAT, NLON, C), 1.0, 6.0, ((0, 4), (1, 8)))
    weight = gaussian(key_list[2], (K, C, C), (K * C) ** -0.5, 0.1875)
    filter_taps = gaussian(key_list[3], (NLAT, K, NDL, 2 * LON_DEV), 1.0, 6.0, ((0, 4),))
    lat_ext = draw_lat_ext(jax.random.fold_in(key_list[6], 71), 0)
    lon_count = draw_lon_count(jax.random.fold_in(key_list[6], 71), 0)
    return dict(features=features, cotangent=cotangent, weight=weight, filter_taps=filter_taps, lat_ext=lat_ext, lon_count=lon_count)


def make_filters(filter_taps, lat_ext, lon_count):
    lat_reach = filter_taps.shape[2] // 2
    half_width = filter_taps.shape[3] // 2
    lat_dist = jnp.abs(jnp.arange(filter_taps.shape[2], dtype=jnp.int32) - lat_reach)
    lon_dist = jnp.abs(jnp.arange(filter_taps.shape[3], dtype=jnp.int32) - half_width)
    support = (lat_dist[None, :, None] < lat_ext[:, None, None]) & (lon_dist[None, None, :] < lon_count[:, None, None])
    support_size = ((2 * lat_ext - 1) * (2 * lon_count - 1)).astype(jnp.float32)
    row_scale = lax.rsqrt(support_size)
    masked = filter_taps.astype(jnp.float32) * support[:, None].astype(jnp.float32) * row_scale[:, None, None, None]
    return masked.astype(jnp.bfloat16)

def reference(features, cotangent, weight, filter_taps, lat_ext, lon_count):
    filters = make_filters(filter_taps, lat_ext, lon_count)
    spread = jnp.concatenate([filters[..., LON_DEV:].astype(jnp.float32), jnp.zeros((NLAT, K, NDL, NLON - 2 * LON_DEV), jnp.float32), filters[..., :LON_DEV].astype(jnp.float32)], axis=-1)
    kernel_spec = jnp.fft.rfft(spread, axis=-1)
    feature_spec = jnp.pad(jnp.fft.rfft(features.astype(jnp.float32), axis=1), ((HLAT, HLAT), (0, 0), (0, 0)))
    flat_cot = cotangent.reshape(NLAT * NLON, C)
    output = jnp.zeros((NLAT * NLON, C), jnp.float32)
    grad_spec = jnp.zeros((NLAT + 2 * HLAT, NLON // 2 + 1, C), kernel_spec.dtype)
    norm_scale = 1.0 / math.sqrt(NLAT * NLON)
    basis_grads = []
    for basis_index in range(K):
        summed = jnp.conj(kernel_spec[:, basis_index, 0])[:, :, None] * feature_spec[0:NLAT]
        for offset in range(1, NDL):
            summed = summed + jnp.conj(kernel_spec[:, basis_index, offset])[:, :, None] * feature_spec[offset:offset + NLAT]
        basis_out = jnp.fft.irfft(summed, n=NLON, axis=1).astype(jnp.bfloat16).reshape(NLAT * NLON, C)
        output = output + jnp.dot(basis_out, weight[basis_index], preferred_element_type=jnp.float32)
        basis_grad = lax.dot_general(flat_cot, weight[basis_index], (((1,), (1,)), ((), ())), preferred_element_type=jnp.float32).astype(jnp.bfloat16)
        partial_grad = lax.dot_general(basis_out, flat_cot, (((0,), (0,)), ((), ())), preferred_element_type=jnp.float32)
        basis_grads.append(partial_grad * norm_scale)
        grad_rows = jnp.fft.rfft(basis_grad.astype(jnp.float32).reshape(NLAT, NLON, C), axis=1)
        for offset in range(NDL):
            grad_spec = grad_spec.at[offset:offset + NLAT].add(kernel_spec[:, basis_index, offset][:, :, None] * grad_rows)
    field_grad = jnp.fft.irfft(grad_spec[HLAT:HLAT + NLAT], n=NLON, axis=1).astype(jnp.bfloat16)
    return (output.astype(jnp.bfloat16).reshape(NLAT, NLON, C), field_grad, jnp.stack(basis_grads))
```

```python
import math

import jax
import jax.numpy as jnp
from jax import lax
from jax.sharding import PartitionSpec as P


def swap(block, axis, offset, closed):
    count = lax.axis_size(axis)
    pairs = []
    for first in range(offset, count, 2):
        second = first + 1
        if second >= count:
            if not closed:
                continue
            second %= count
        pairs += [(first, second), (second, first)]
    return lax.ppermute(block, axis, pairs)


def flip(block, axis, bit):
    count = lax.axis_size(axis)
    return lax.ppermute(block, axis, [(i, i ^ bit) for i in range(count)])


def make_filters(filter_taps, lat_ext, lon_count):
    lat_reach = filter_taps.shape[2] // 2
    half_width = filter_taps.shape[3] // 2
    lat_dist = jnp.abs(jnp.arange(filter_taps.shape[2], dtype=jnp.int32) - lat_reach)
    lon_dist = jnp.abs(jnp.arange(filter_taps.shape[3], dtype=jnp.int32) - half_width)
    support = (lat_dist[None, :, None] < lat_ext[:, None, None]) & (
        lon_dist[None, None, :] < lon_count[:, None, None]
    )
    support_size = ((2 * lat_ext - 1) * (2 * lon_count - 1)).astype(jnp.float32)
    row_scale = lax.rsqrt(support_size)
    masked = (
        filter_taps.astype(jnp.float32)
        * support[:, None].astype(jnp.float32)
        * row_scale[:, None, None, None]
    )
    return masked.astype(jnp.bfloat16)


def band_matrix(taps, lon_width, lead):
    leading = taps.shape[:-1]
    padded = jnp.concatenate(
        [
            jnp.zeros(leading + (lead,), taps.dtype),
            taps,
            jnp.zeros(leading + (lon_width + 1 - lead,), taps.dtype),
        ],
        axis=-1,
    )
    repeated = jnp.tile(padded, (1,) * len(leading) + (lon_width,))
    return repeated[..., : lon_width * 3 * lon_width].reshape(leading + (lon_width, 3 * lon_width))


def halves(block, bit_set):
    half = block.shape[0] // 2
    keep = lax.dynamic_slice_in_dim(block, bit_set * half, half, 0)
    send = lax.dynamic_slice_in_dim(block, (1 - bit_set) * half, half, 0)
    return keep, send


def all_reduce(partial):
    lat, lon = lax.axis_index("lat"), lax.axis_index("lon")
    lat_bits = [1 << b for b in range(lax.axis_size("lat").bit_length() - 1)]
    lon_bits = [1 << b for b in range(lax.axis_size("lon").bit_length() - 1)]
    scatter = [("lat", lat, b) for b in lat_bits] + [("lon", lon, lon_bits[0])]
    value = partial
    for axis, index, bit in scatter:
        keep, send = halves(value, (index // bit) % 2)
        got = flip(send.astype(jnp.bfloat16), axis, bit)
        value = keep + got.astype(jnp.float32)
    for bit in lon_bits[1:]:
        mine = value.astype(jnp.bfloat16)
        got = flip(mine, "lon", bit)
        value = mine.astype(jnp.float32) + got.astype(jnp.float32)
    whole = value.astype(jnp.bfloat16)
    for axis, index, bit in scatter[::-1]:
        got = flip(whole, axis, bit)
        upper = (index // bit) % 2 == 1
        whole = jnp.concatenate([jnp.where(upper, got, whole), jnp.where(upper, whole, got)], axis=0)
    return whole


def per_device(features, cotangent, weight, filter_taps, lat_ext, lon_count):
    row_count, lon_width, channels = features.shape
    basis_count = weight.shape[0]
    lat_taps = filter_taps.shape[2]
    lat_reach = lat_taps // 2
    lat, lon = lax.axis_index("lat"), lax.axis_index("lon")
    filters = make_filters(filter_taps, lat_ext, lon_count)

    own = jnp.concatenate([features, cotangent], axis=0)
    far = swap(own, "lon", 1, True)
    near = swap(own, "lon", 0, True)
    lon_even = lon % 2 == 0
    west = jnp.where(lon_even, far, near)
    east = jnp.where(lon_even, near, far)
    strip = jnp.concatenate([west, own, east], axis=1).reshape(
        2, row_count, 3 * lon_width, channels
    )

    lat_even = lat % 2 == 0

    def edge(array, axis, bottom):
        start = jnp.where(bottom, row_count - lat_reach, 0)
        return lax.dynamic_slice_in_dim(array, start, lat_reach, axis)

    filter_size = lat_reach * basis_count * lat_taps * filter_taps.shape[3]
    filter_rows = -(-filter_size // (16 * channels)) * 16

    def message(bottom):
        cells = edge(strip, 1, bottom).reshape(-1, channels)
        taps = edge(filters, 0, bottom).reshape(-1)
        taps = jnp.pad(taps, (0, filter_rows * channels - filter_size)).reshape(-1, channels)
        return jnp.concatenate([cells, taps], axis=0)

    across = swap(message(jnp.logical_not(lat_even)), "lat", 1, False)
    beside = swap(message(lat_even), "lat", 0, False)
    north = jnp.where(lat_even, across, beside)
    south = jnp.where(lat_even, beside, across)

    def unpack(rows):
        cells = rows[:-filter_rows].reshape(2, lat_reach, 3 * lon_width, channels)
        taps = rows[-filter_rows:].reshape(-1)[:filter_size]
        return cells, taps.reshape((lat_reach,) + filter_taps.shape[1:])

    north_cells, north_taps = unpack(north)
    south_cells, south_taps = unpack(south)
    window = jnp.concatenate([north_cells, strip, south_cells], axis=1)
    all_taps = jnp.concatenate([north_taps, filters, south_taps], axis=0)

    banded = band_matrix(filters, lon_width, 0)
    patches = jnp.stack([window[0, e : e + row_count] for e in range(lat_taps)], axis=1)
    basis_f32 = jnp.einsum("okejm,oemc->ojkc", banded, patches, preferred_element_type=jnp.float32)
    flat_out = basis_f32.astype(jnp.bfloat16).reshape(row_count * lon_width, basis_count * channels)
    flat_weight = weight.reshape(basis_count * channels, channels)
    flat_cot = cotangent.reshape(row_count * lon_width, channels)
    partial_grad = lax.dot_general(
        flat_out, flat_cot, (((0,), (0,)), ((), ())), preferred_element_type=jnp.float32
    )
    total_cells = row_count * lax.axis_size("lat") * lon_width * lax.axis_size("lon")
    weight_grad = all_reduce(partial_grad * (1.0 / math.sqrt(total_cells)))
    weight_grad = weight_grad.astype(jnp.float32).reshape(basis_count, channels, channels)

    output = jnp.dot(flat_out, flat_weight, preferred_element_type=jnp.float32).astype(jnp.bfloat16)
    output = output.reshape(row_count, lon_width, channels)

    turned = jnp.stack(
        [all_taps[lat_taps - 1 - e : lat_taps - 1 - e + row_count, :, e] for e in range(lat_taps)], axis=2
    )[..., ::-1]
    grad_banded = band_matrix(turned, lon_width, 1)
    grad_patches = jnp.stack(
        [window[1, lat_taps - 1 - e : lat_taps - 1 - e + row_count] for e in range(lat_taps)], axis=1
    )
    spread = jnp.einsum(
        "okejm,oemc->ojkc", grad_banded, grad_patches, preferred_element_type=jnp.float32
    ).astype(jnp.bfloat16)
    turned_weight = jnp.swapaxes(weight, 1, 2).reshape(basis_count * channels, channels)
    field_grad = jnp.dot(
        spread.reshape(row_count * lon_width, basis_count * channels),
        turned_weight,
        preferred_element_type=jnp.float32,
    ).astype(jnp.bfloat16)
    field_grad = field_grad.reshape(row_count, lon_width, channels)
    return (output, field_grad, weight_grad)


def solution(mesh):
    in_specs = (
        P("lat", "lon", None),
        P("lat", "lon", None),
        P(),
        P("lat", None, None, None),
        P("lat"),
        P("lat"),
    )
    out_specs = (P("lat", "lon", None), P("lat", "lon", None), P())
    return jax.shard_map(
        per_device, mesh=mesh, in_specs=in_specs, out_specs=out_specs, check_vma=False
    )
```

```python
import functools
import math

import jax
import jax.numpy as jnp
from jax import lax
from jax.experimental import pallas as pl
from jax.experimental.pallas import tpu as pltpu
from jax.sharding import PartitionSpec as P

LANES = 128
TAP_ROWS = 8


def shift(block, axis, by):
    count = lax.axis_size(axis)
    return lax.ppermute(block, axis, [(i, (i + by) % count) for i in range(count)])


def flip(block, axis, bit):
    count = lax.axis_size(axis)
    return lax.ppermute(block, axis, [(i, i ^ bit) for i in range(count)])


def outer_swap(block, axis):
    count = lax.axis_size(axis)
    pairs = [(i, i + 1) for i in range(1, count - 1, 2)]
    return lax.ppermute(block, axis, pairs + [(b, a) for a, b in pairs])


def make_filters(filter_taps, lat_ext, lon_count):
    lat_reach = filter_taps.shape[2] // 2
    half_width = filter_taps.shape[3] // 2
    lat_dist = jnp.abs(jnp.arange(filter_taps.shape[2], dtype=jnp.int32) - lat_reach)
    lon_dist = jnp.abs(jnp.arange(filter_taps.shape[3], dtype=jnp.int32) - half_width)
    support = (lat_dist[None, :, None] < lat_ext[:, None, None]) & (
        lon_dist[None, None, :] < lon_count[:, None, None]
    )
    support_size = ((2 * lat_ext - 1) * (2 * lon_count - 1)).astype(jnp.float32)
    row_scale = lax.rsqrt(support_size)
    masked = (
        filter_taps.astype(jnp.float32)
        * support[:, None].astype(jnp.float32)
        * row_scale[:, None, None, None]
    )
    return masked.astype(jnp.bfloat16)


class Layout:
    def __init__(self, rows, reach, width, basis, channels):
        self.rows, self.reach, self.width = rows, reach, width
        self.basis, self.channels = basis, channels
        self.taps = 2 * reach + 1
        self.own = rows + reach
        self.total = 3 * rows + 2 * reach
        self.domain = 2 * rows + reach
        self.strip = 3 * width
        self.cells = 2 * rows * self.strip
        self.edge_cells = 2 * reach * self.strip

    def places(self, even):
        partner = jnp.where(even, self.own + self.rows, self.own - self.rows)
        outer = jnp.where(even, self.own - self.reach, self.own + self.rows)
        first = jnp.where(even, self.own - self.reach, self.own - self.rows)
        return partner, outer, first


def fill(lay, even, strip, partner, outer, window, taps):
    at_partner, at_outer, _ = lay.places(even)
    rows, reach, cols = lay.rows, lay.reach, lay.strip
    window[...] = jnp.zeros_like(window)
    for field in range(2):
        for row in range(rows):
            window[field, lay.own + row, :cols] = strip[field, row]
            start = (field * rows + row) * cols
            window[field, at_partner + row, :cols] = partner[start : start + cols]
        for row in range(reach):
            start = (field * reach + row) * cols
            window[field, at_outer + row, :cols] = outer[start : start + cols]


def fill_taps(lay, even, own, partner, outer, taps):
    at_partner, at_outer, _ = lay.places(even)
    per_row = lay.basis * TAP_ROWS
    taps[...] = jnp.zeros_like(taps)
    for row in range(lay.rows):
        taps[lay.own + row] = own[row * per_row : (row + 1) * per_row].astype(jnp.float32)
        start = lay.cells + row * per_row
        taps[at_partner + row] = partner[start : start + per_row].astype(jnp.float32)
    for row in range(lay.reach):
        start = lay.edge_cells + row * per_row
        taps[at_outer + row] = outer[start : start + per_row].astype(jnp.float32)


def weight_kernel(lay, scale, strip, filters, partner, outer, grad, window, taps, basis_out):
    lat, lon = lax.axis_index("lat"), lax.axis_index("lon")
    even, lon_even = lat % 2 == 0, lon % 2 == 0
    mine = (lat % 2) * 2 + lon % 2
    fill(lay, even, strip, partner, outer, window, taps)
    fill_taps(lay, even, filters, partner, outer, taps)
    _, _, first = lay.places(even)
    width, reach = lay.width, lay.reach
    lane = lax.broadcasted_iota(jnp.int32, (1, LANES), 1)
    keep_west = jnp.where((lane < width) & lon_even, 0.0, 1.0)
    keep_east = jnp.where((lane >= 2 * width) & jnp.logical_not(lon_even), 0.0, 1.0)
    at_mine = pl.multiple_of(mine * TAP_ROWS, TAP_ROWS)
    for row in range(lay.domain):
        blocks = []
        lines = taps[first + row, pl.ds(at_mine, TAP_ROWS), :LANES]
        for e in range(lay.taps):
            line = lines[e : e + 1]
            source = row + e - reach
            if row < reach and 0 <= source < reach:
                line = jnp.where(even, 0.0, line)
            tail = lay.domain - reach
            if row >= tail and tail <= source < lay.domain:
                line = jnp.where(even, line, 0.0)
            spread = jnp.broadcast_to(line, (width, LANES))
            middle = pltpu.roll(spread, 0, 1, stride=1, stride_axis=0)
            west = pltpu.roll(middle, LANES - width, 1) * keep_west
            east = pltpu.roll(middle, width, 1) * keep_east
            blocks.append(jnp.concatenate([west, middle, east], axis=0).astype(jnp.bfloat16))
        band = jnp.concatenate(blocks, axis=1)
        source = window[0, pl.ds(first + row - reach, lay.taps)].reshape(lay.taps * LANES, lay.channels)
        result = jnp.dot(band, source, preferred_element_type=jnp.float32)
        basis_out[row * lay.strip : (row + 1) * lay.strip] = result.astype(jnp.bfloat16)
    cot = window[1, pl.ds(first, lay.domain), : lay.strip].reshape(lay.domain * lay.strip, lay.channels)
    total = lax.dot_general(
        basis_out[...], cot, (((0,), (0,)), ((), ())), preferred_element_type=jnp.float32
    )
    grad[...] = (total * scale).astype(jnp.bfloat16)


def field_kernel(lay, strip, filters, partner, outer, weight, output, field_grad, window, taps, mixed):
    even = lax.axis_index("lat") % 2 == 0
    fill(lay, even, strip, partner, outer, window, taps)
    fill_taps(lay, even, filters, partner, outer, taps)
    width, reach, rows, basis = lay.width, lay.reach, lay.rows, lay.basis

    def bands(row, turned):
        blocks = []
        for n in range(lay.taps):
            at, e = (row + n - reach, lay.taps - 1 - n) if turned else (row, n)
            lanes = slice(LANES, 2 * LANES) if turned else slice(0, LANES)
            parts = []
            for k in range(basis):
                line = taps[lay.own + at, k * TAP_ROWS + e : k * TAP_ROWS + e + 1, lanes]
                spread = jnp.broadcast_to(line, (width, LANES))
                parts.append(pltpu.roll(spread, int(turned), 1, stride=1, stride_axis=0))
            blocks.append(jnp.concatenate(parts, axis=0).astype(jnp.bfloat16))
        return jnp.concatenate(blocks, axis=1)

    for field, turned, out in ((0, False, output), (1, True, field_grad)):
        for row in range(rows):
            source = window[field, lay.own + row - reach : lay.own + row + reach + 1]
            source = source.reshape(lay.taps * LANES, lay.channels)
            result = jnp.dot(bands(row, turned), source, preferred_element_type=jnp.float32)
            result = result.astype(jnp.bfloat16)
            for k in range(basis):
                mixed[k, row * width : (row + 1) * width] = result[k * width : (k + 1) * width]
        total = jnp.zeros((rows * width, lay.channels), jnp.float32)
        for k in range(basis):
            dims = (((1,), (1,)), ((), ())) if turned else (((1,), (0,)), ((), ()))
            total += lax.dot_general(mixed[k], weight[k], dims, preferred_element_type=jnp.float32)
        out[...] = total.astype(jnp.bfloat16).reshape(out.shape)


def per_device(features, cotangent, weight, filter_taps, lat_ext, lon_count):
    rows, width, channels = features.shape
    basis = weight.shape[0]
    lat_taps = filter_taps.shape[2]
    lay = Layout(rows, lat_taps // 2, width, basis, channels)
    lat, lon = lax.axis_index("lat"), lax.axis_index("lon")
    even = lat % 2 == 0

    filters = make_filters(filter_taps, lat_ext, lon_count)
    gap = jnp.zeros(filters.shape[:-1] + (LANES - filters.shape[-1],), filters.dtype)
    filters = jnp.concatenate([filters, gap, filters[..., ::-1], gap], axis=-1)
    filters = jnp.pad(filters, ((0, 0), (0, 0), (0, TAP_ROWS - lat_taps), (0, 0)))
    per_row = basis * TAP_ROWS
    filters = filters.reshape(rows * per_row, 2 * LANES)

    own = jnp.concatenate([features, cotangent], axis=0)
    west = shift(own, "lon", 1)
    east = shift(own, "lon", -1)
    strip = jnp.concatenate([west, own, east], axis=1).reshape(2, rows, lay.strip, channels)

    def edge(array, axis, size, bottom):
        start = jnp.where(bottom, array.shape[axis] - size, 0)
        return lax.dynamic_slice_in_dim(array, start, size, axis)

    outward = jnp.concatenate(
        [
            edge(strip, 1, lay.reach, jnp.logical_not(even)).reshape(-1, channels),
            edge(filters, 0, lay.reach * per_row, jnp.logical_not(even)),
        ],
        axis=0,
    )
    outer = outer_swap(outward, "lat")
    partner = flip(jnp.concatenate([strip.reshape(-1, channels), filters], axis=0), "lat", 1)

    vmem = pl.BlockSpec(memory_space=pltpu.VMEM)
    window_shape = pltpu.VMEM((2, lay.total, LANES, channels), jnp.bfloat16)
    taps_shape = pltpu.VMEM((lay.total, per_row, 2 * LANES), jnp.float32)
    total_cells = rows * lax.axis_size("lat") * width * lax.axis_size("lon")
    grad = pl.pallas_call(
        functools.partial(weight_kernel, lay, 1.0 / math.sqrt(total_cells)),
        out_shape=jax.ShapeDtypeStruct((channels, channels), jnp.bfloat16),
        in_specs=[vmem] * 4,
        out_specs=vmem,
        scratch_shapes=[
            window_shape,
            taps_shape,
            pltpu.VMEM((lay.domain * lay.strip, channels), jnp.bfloat16),
        ],
        compiler_params=pltpu.CompilerParams(vmem_limit_bytes=32 * 1024 * 1024),
        cost_estimate=pl.CostEstimate(flops=400_000_000, bytes_accessed=3_000_000, transcendentals=0),
        name="weight_partial",
    )(strip, filters, partner, outer)

    output, field_grad = pl.pallas_call(
        functools.partial(field_kernel, lay),
        out_shape=[jax.ShapeDtypeStruct(features.shape, jnp.bfloat16)] * 2,
        in_specs=[vmem] * 5,
        out_specs=[vmem] * 2,
        scratch_shapes=[
            window_shape,
            taps_shape,
            pltpu.VMEM((basis, rows * width, channels), jnp.bfloat16),
        ],
        compiler_params=pltpu.CompilerParams(vmem_limit_bytes=32 * 1024 * 1024),
        cost_estimate=pl.CostEstimate(flops=400_000_000, bytes_accessed=3_000_000, transcendentals=0),
        name="fields",
    )(strip, filters, partner, outer, weight)

    others = [("lat", 1 << b) for b in range(1, lax.axis_size("lat").bit_length() - 1)]
    others += [("lon", 1 << b) for b in range(1, lax.axis_size("lon").bit_length() - 1)]
    for axis, bit in others:
        total = grad.astype(jnp.float32) + flip(grad, axis, bit).astype(jnp.float32)
        grad = total.astype(jnp.bfloat16)
    for axis, index in (("lon", lon), ("lat", lat)):
        got = flip(grad, axis, 1)
        upper = index % 2 == 1
        grad = jnp.concatenate([jnp.where(upper, got, grad), jnp.where(upper, grad, got)], axis=0)
    weight_grad = grad.astype(jnp.float32).reshape(basis, channels, channels)
    return (output, field_grad, weight_grad)


def solution(mesh):
    in_specs = (
        P("lat", "lon", None),
        P("lat", "lon", None),
        P(),
        P("lat", None, None, None),
        P("lat"),
        P("lat"),
    )
    out_specs = (P("lat", "lon", None), P("lat", "lon", None), P())
    return jax.shard_map(
        per_device, mesh=mesh, in_specs=in_specs, out_specs=out_specs, check_vma=False
    )
```

```python
import functools
import math

import jax
import jax.numpy as jnp
from jax import lax
from jax.experimental import pallas as pl
from jax.experimental.pallas import tpu as pltpu
from jax.sharding import PartitionSpec as P

LANES = 128
INNER_FLOPS = 300_000_000
TAP_ROWS = 8


def shift(block, axis, by):
    count = lax.axis_size(axis)
    return lax.ppermute(block, axis, [(i, (i + by) % count) for i in range(count)])


def flip(block, axis, bit):
    count = lax.axis_size(axis)
    return lax.ppermute(block, axis, [(i, i ^ bit) for i in range(count)])


def outer_swap(block, axis):
    count = lax.axis_size(axis)
    pairs = [(i, i + 1) for i in range(1, count - 1, 2)]
    return lax.ppermute(block, axis, pairs + [(b, a) for a, b in pairs])


def make_filters(filter_taps, lat_ext, lon_count, row_scale):
    lat_reach = filter_taps.shape[2] // 2
    half_width = filter_taps.shape[3] // 2
    lat_dist = jnp.abs(jnp.arange(filter_taps.shape[2], dtype=jnp.int32) - lat_reach)
    lon_dist = jnp.abs(jnp.arange(filter_taps.shape[3], dtype=jnp.int32) - half_width)
    support = (lat_dist[None, :, None] < lat_ext[:, None, None]) & (
        lon_dist[None, None, :] < lon_count[:, None, None]
    )
    masked = (
        filter_taps.astype(jnp.float32)
        * support[:, None].astype(jnp.float32)
        * row_scale[:, None, None, None]
    )
    return masked.astype(jnp.bfloat16)


class Layout:
    def __init__(self, rows, reach, width, basis, channels):
        self.rows, self.reach, self.width = rows, reach, width
        self.basis, self.channels = basis, channels
        self.taps = 2 * reach + 1
        self.strip = 3 * width
        self.per_row = basis * TAP_ROWS
        self.cells = 2 * rows * self.strip
        self.edge_cells = 2 * reach * self.strip


def put_row(lay, window, field, at, cells):
    window[field, at, : lay.strip] = cells
    window[field, at, lay.strip :] = jnp.zeros((LANES - lay.strip, lay.channels), jnp.bfloat16)


def message_row(lay, message, rows, field, row):
    start = (field * rows + row) * lay.strip
    return message[start : start + lay.strip]


def message_taps(lay, message, rows, row):
    start = 2 * rows * lay.strip + row * lay.per_row
    return message[start : start + lay.per_row].astype(jnp.float32)


def own_taps(lay, filters, row):
    return filters[row * lay.per_row : (row + 1) * lay.per_row].astype(jnp.float32)


def my_basis():
    return (lax.axis_index("lat") % 2) * 2 + lax.axis_index("lon") % 2


def strip_band(lay, line, keep_west, keep_east):
    width = lay.width
    middle = pltpu.roll(jnp.broadcast_to(line, (width, LANES)), 0, 1, stride=1, stride_axis=0)
    west = pltpu.roll(middle, LANES - width, 1) * keep_west
    east = pltpu.roll(middle, width, 1) * keep_east
    return jnp.concatenate([west, middle, east], axis=0).astype(jnp.bfloat16)


def keep_lanes(lay):
    even = lax.axis_index("lon") % 2 == 0
    lane = lax.broadcasted_iota(jnp.int32, (1, LANES), 1)
    west = jnp.where((lane < lay.width) & even, 0.0, 1.0)
    east = jnp.where((lane >= 2 * lay.width) & jnp.logical_not(even), 0.0, 1.0)
    return west, east


def product(left, right, dims):
    return lax.dot_general(left, right, (dims, ((), ())), preferred_element_type=jnp.float32)


def inner_kernel(lay, strip, filters, partner, grad, window, taps, basis_out):
    rows, reach = lay.rows, lay.reach
    even = lax.axis_index("lat") % 2 == 0
    at_own, at_partner = jnp.where(even, 0, rows), jnp.where(even, rows, 0)
    for row in range(rows):
        for field in range(2):
            put_row(lay, window, field, at_own + row, strip[field, row])
            put_row(lay, window, field, at_partner + row, message_row(lay, partner, rows, field, row))
        taps[at_own + row] = own_taps(lay, filters, row)
        taps[at_partner + row] = message_taps(lay, partner, rows, row)
    keep_west, keep_east = keep_lanes(lay)
    at_mine = pl.multiple_of(my_basis() * TAP_ROWS, TAP_ROWS)
    for row in range(2 * rows):
        lines = taps[row, pl.ds(at_mine, TAP_ROWS), :LANES]
        low, high = max(0, row - reach), min(2 * rows, row + reach + 1)
        bands = [
            strip_band(lay, lines[e : e + 1], keep_west, keep_east)
            for e in range(low - row + reach, high - row + reach)
        ]
        source = window[0, low:high].reshape((high - low) * LANES, lay.channels)
        result = product(jnp.concatenate(bands, axis=1), source, ((1,), (0,)))
        basis_out[row * lay.strip : (row + 1) * lay.strip] = result.astype(jnp.bfloat16)
    cot = window[1, :, : lay.strip].reshape(2 * rows * lay.strip, lay.channels)
    grad[...] = product(basis_out[...], cot, ((0,), (0,)))


def outer_kernel(lay, scale, strip, filters, outer, inner, grad, window, taps, basis_out):
    rows, reach = lay.rows, lay.reach
    even = lax.axis_index("lat") % 2 == 0
    at_outer, at_own = jnp.where(even, 0, reach), jnp.where(even, reach, 0)
    first = jnp.where(even, 0, rows - reach)
    for row in range(reach):
        for field in range(2):
            put_row(lay, window, field, at_own + row, strip[field, first + row])
            put_row(lay, window, field, at_outer + row, message_row(lay, outer, reach, field, row))
        taps[at_outer + row] = message_taps(lay, outer, reach, row)
        taps[at_own + row] = jnp.where(
            even, own_taps(lay, filters, row), own_taps(lay, filters, rows - reach + row)
        )
    keep_west, keep_east = keep_lanes(lay)
    at_mine = pl.multiple_of(my_basis() * TAP_ROWS, TAP_ROWS)
    nothing = jnp.zeros((lay.strip, LANES), jnp.bfloat16)
    for side in range(2):
        rows_of_bands = []
        for row in range(side * reach, (side + 1) * reach):
            lines = taps[row, pl.ds(at_mine, TAP_ROWS), :LANES]
            blocks = []
            for other in range((1 - side) * reach, (2 - side) * reach):
                e = other - row + reach
                inside = 0 <= e < lay.taps
                blocks.append(
                    strip_band(lay, lines[e : e + 1], keep_west, keep_east) if inside else nothing
                )
            rows_of_bands.append(jnp.concatenate(blocks, axis=1))
        source = window[0, (1 - side) * reach : (2 - side) * reach]
        result = product(
            jnp.concatenate(rows_of_bands, axis=0),
            source.reshape(reach * LANES, lay.channels),
            ((1,), (0,)),
        )
        start = side * reach * lay.strip
        basis_out[start : start + reach * lay.strip] = result.astype(jnp.bfloat16)
    cot = window[1, :, : lay.strip].reshape(2 * reach * lay.strip, lay.channels)
    total = inner[...] + product(basis_out[...], cot, ((0,), (0,)))
    grad[...] = (total * scale).astype(jnp.bfloat16)


def field_kernel(lay, strip, filters, partner, outer, weight, output, field_grad, window, taps, mixed):
    rows, reach, width, basis = lay.rows, lay.reach, lay.width, lay.basis
    even = lax.axis_index("lat") % 2 == 0
    at_outer, at_partner = jnp.where(even, 0, rows + reach), jnp.where(even, rows + reach, 0)
    for field in range(2):
        for row in range(rows):
            put_row(lay, window, field, reach + row, strip[field, row])
        for row in range(reach):
            near = jnp.where(
                even,
                message_row(lay, partner, rows, field, row),
                message_row(lay, partner, rows, field, rows - reach + row),
            )
            put_row(lay, window, field, at_partner + row, near)
            put_row(lay, window, field, at_outer + row, message_row(lay, outer, reach, field, row))
    for row in range(rows):
        taps[reach + row] = own_taps(lay, filters, row)
    for row in range(reach):
        taps[at_partner + row] = jnp.where(
            even,
            message_taps(lay, partner, rows, row),
            message_taps(lay, partner, rows, rows - reach + row),
        )
        taps[at_outer + row] = message_taps(lay, outer, reach, row)

    def bands(row, turned):
        blocks = []
        for n in range(lay.taps):
            at, e = (row + n, lay.taps - 1 - n) if turned else (reach + row, n)
            lanes = slice(LANES, 2 * LANES) if turned else slice(0, LANES)
            parts = []
            for k in range(basis):
                line = taps[at, k * TAP_ROWS + e : k * TAP_ROWS + e + 1, lanes]
                spread = jnp.broadcast_to(line, (width, LANES))
                parts.append(pltpu.roll(spread, int(turned), 1, stride=1, stride_axis=0))
            blocks.append(jnp.concatenate(parts, axis=0).astype(jnp.bfloat16))
        return jnp.concatenate(blocks, axis=1)

    for field, turned, out in ((0, False, output), (1, True, field_grad)):
        for row in range(rows):
            source = window[field, row : row + lay.taps].reshape(lay.taps * LANES, lay.channels)
            result = product(bands(row, turned), source, ((1,), (0,))).astype(jnp.bfloat16)
            for k in range(basis):
                mixed[k, row * width : (row + 1) * width] = result[k * width : (k + 1) * width]
        total = jnp.zeros((rows * width, lay.channels), jnp.float32)
        for k in range(basis):
            total += product(mixed[k], weight[k], ((1,), (1 if turned else 0,)))
        out[...] = total.astype(jnp.bfloat16).reshape(out.shape)


def call(kernel, outs, scratch, flops, name):
    vmem = pl.BlockSpec(memory_space=pltpu.VMEM)

    def run(*operands):
        return pl.pallas_call(
            kernel,
            out_shape=outs,
            in_specs=[vmem] * len(operands),
            out_specs=[vmem] * len(outs),
            scratch_shapes=scratch,
            compiler_params=pltpu.CompilerParams(vmem_limit_bytes=32 * 1024 * 1024),
            cost_estimate=pl.CostEstimate(flops=flops, bytes_accessed=1_000_000, transcendentals=0),
            name=name,
        )(*operands)

    return run


def per_device(features, cotangent, weight, filter_taps, lat_ext, lon_count):
    rows, width, channels = features.shape
    basis = weight.shape[0]
    lat_taps = filter_taps.shape[2]
    lay = Layout(rows, lat_taps // 2, width, basis, channels)
    lat, lon = lax.axis_index("lat"), lax.axis_index("lon")
    even = lat % 2 == 0

    own = jnp.concatenate([features, cotangent], axis=0)
    west = shift(own, "lon", 1)
    support_size = ((2 * lat_ext - 1) * (2 * lon_count - 1)).astype(jnp.float32)
    own, row_scale = lax.optimization_barrier((own, lax.rsqrt(support_size)))
    east = shift(own, "lon", -1)
    filters = make_filters(filter_taps, lat_ext, lon_count, row_scale)
    gap = jnp.zeros(filters.shape[:-1] + (LANES - filters.shape[-1],), filters.dtype)
    filters = jnp.concatenate([filters, gap, filters[..., ::-1], gap], axis=-1)
    filters = jnp.pad(filters, ((0, 0), (0, 0), (0, TAP_ROWS - lat_taps), (0, 0)))
    per_row = basis * TAP_ROWS
    filters = filters.reshape(rows * per_row, 2 * LANES)

    strip = jnp.concatenate([west, own, east], axis=1).reshape(2, rows, lay.strip, channels)

    def edge(array, axis, size, bottom):
        start = jnp.where(bottom, array.shape[axis] - size, 0)
        return lax.dynamic_slice_in_dim(array, start, size, axis)

    outward = jnp.concatenate(
        [
            edge(strip, 1, lay.reach, jnp.logical_not(even)).reshape(-1, channels),
            edge(filters, 0, lay.reach * per_row, jnp.logical_not(even)),
        ],
        axis=0,
    )
    outer = outer_swap(outward, "lat")
    partner = flip(jnp.concatenate([strip.reshape(-1, channels), filters], axis=0), "lat", 1)

    def scratch(window_rows, basis_rows):
        return [
            pltpu.VMEM((2, window_rows, LANES, channels), jnp.bfloat16),
            pltpu.VMEM((window_rows, per_row, 2 * LANES), jnp.float32),
            pltpu.VMEM((basis_rows, channels), jnp.bfloat16),
        ]

    total_cells = rows * lax.axis_size("lat") * width * lax.axis_size("lon")
    (inner,) = call(
        functools.partial(inner_kernel, lay),
        [jax.ShapeDtypeStruct((channels, channels), jnp.float32)],
        scratch(2 * rows, 2 * rows * lay.strip),
        INNER_FLOPS,
        "weight_inner",
    )(strip, filters, partner)
    (grad,) = call(
        functools.partial(outer_kernel, lay, 1.0 / math.sqrt(total_cells)),
        [jax.ShapeDtypeStruct((channels, channels), jnp.bfloat16)],
        scratch(2 * lay.reach, 2 * lay.reach * lay.strip),
        100_000_000,
        "weight_outer",
    )(strip, filters, outer, inner)
    output, field_grad = call(
        functools.partial(field_kernel, lay),
        [jax.ShapeDtypeStruct(features.shape, jnp.bfloat16)] * 2,
        scratch(rows + 2 * lay.reach, 0)[:2]
        + [pltpu.VMEM((basis, rows * width, channels), jnp.bfloat16)],
        400_000_000,
        "fields",
    )(strip, filters, partner, outer, weight)

    others = [("lat", 1 << b) for b in range(1, lax.axis_size("lat").bit_length() - 1)]
    others += [("lon", 1 << b) for b in range(1, lax.axis_size("lon").bit_length() - 1)]
    for axis, bit in others:
        total = grad.astype(jnp.float32) + flip(grad, axis, bit).astype(jnp.float32)
        grad = total.astype(jnp.bfloat16)
    for axis, index in (("lon", lon), ("lat", lat)):
        got = flip(grad, axis, 1)
        upper = index % 2 == 1
        grad = jnp.concatenate([jnp.where(upper, got, grad), jnp.where(upper, grad, got)], axis=0)
    weight_grad = grad.astype(jnp.float32).reshape(basis, channels, channels)
    return (output, field_grad, weight_grad)


def solution(mesh):
    in_specs = (
        P("lat", "lon", None),
        P("lat", "lon", None),
        P(),
        P("lat", None, None, None),
        P("lat"),
        P("lat"),
    )
    out_specs = (P("lat", "lon", None), P("lat", "lon", None), P())
    return jax.shard_map(
        per_device, mesh=mesh, in_specs=in_specs, out_specs=out_specs, check_vma=False
    )
```

```python
import functools
import math

import jax
import jax.numpy as jnp
from jax import lax
from jax.experimental import pallas as pl
from jax.experimental.pallas import tpu as pltpu
from jax.sharding import PartitionSpec as P

LANES = 128
INNER_FLOPS = 300_000_000
MIDDLE_FLOPS = 100_000_000
TAP_ROWS = 8


def shift(block, axis, by):
    count = lax.axis_size(axis)
    return lax.ppermute(block, axis, [(i, (i + by) % count) for i in range(count)])


def flip(block, axis, bit):
    count = lax.axis_size(axis)
    return lax.ppermute(block, axis, [(i, i ^ bit) for i in range(count)])


def outer_swap(block, axis):
    count = lax.axis_size(axis)
    pairs = [(i, i + 1) for i in range(1, count - 1, 2)]
    return lax.ppermute(block, axis, pairs + [(b, a) for a, b in pairs])


def make_filters(filter_taps, lat_ext, lon_count, row_scale):
    lat_reach = filter_taps.shape[2] // 2
    half_width = filter_taps.shape[3] // 2
    lat_dist = jnp.abs(jnp.arange(filter_taps.shape[2], dtype=jnp.int32) - lat_reach)
    lon_dist = jnp.abs(jnp.arange(filter_taps.shape[3], dtype=jnp.int32) - half_width)
    support = (lat_dist[None, :, None] < lat_ext[:, None, None]) & (
        lon_dist[None, None, :] < lon_count[:, None, None]
    )
    masked = (
        filter_taps.astype(jnp.float32)
        * support[:, None].astype(jnp.float32)
        * row_scale[:, None, None, None]
    )
    return masked.astype(jnp.bfloat16)


class Layout:
    def __init__(self, rows, reach, width, basis, channels):
        self.rows, self.reach, self.width = rows, reach, width
        self.basis, self.channels = basis, channels
        self.taps = 2 * reach + 1
        self.strip = 3 * width
        self.per_row = basis * TAP_ROWS
        self.cells = 2 * rows * self.strip
        self.edge_cells = 2 * reach * self.strip


def put_row(lay, window, field, at, cells):
    window[field, at, : lay.strip] = cells
    window[field, at, lay.strip :] = jnp.zeros((LANES - lay.strip, lay.channels), jnp.bfloat16)


def message_row(lay, message, rows, field, row):
    start = (field * rows + row) * lay.strip
    return message[start : start + lay.strip]


def message_taps(lay, message, rows, row):
    start = 2 * rows * lay.strip + row * lay.per_row
    return message[start : start + lay.per_row].astype(jnp.float32)


def own_taps(lay, filters, row):
    return filters[row * lay.per_row : (row + 1) * lay.per_row].astype(jnp.float32)


def my_basis():
    return (lax.axis_index("lat") % 2) * 2 + lax.axis_index("lon") % 2


def strip_band(lay, line, keep_west, keep_east):
    width = lay.width
    middle = pltpu.roll(jnp.broadcast_to(line, (width, LANES)), 0, 1, stride=1, stride_axis=0)
    west = pltpu.roll(middle, LANES - width, 1) * keep_west
    east = pltpu.roll(middle, width, 1) * keep_east
    return jnp.concatenate([west, middle, east], axis=0).astype(jnp.bfloat16)


def keep_lanes(lay):
    even = lax.axis_index("lon") % 2 == 0
    lane = lax.broadcasted_iota(jnp.int32, (1, LANES), 1)
    west = jnp.where((lane < lay.width) & even, 0.0, 1.0)
    east = jnp.where((lane >= 2 * lay.width) & jnp.logical_not(even), 0.0, 1.0)
    return west, east


def product(left, right, dims):
    return lax.dot_general(left, right, (dims, ((), ())), preferred_element_type=jnp.float32)


def inner_kernel(lay, scale, strip, filters, partner, grad, window, taps, basis_out):
    rows, reach = lay.rows, lay.reach
    even = lax.axis_index("lat") % 2 == 0
    at_own, at_partner = jnp.where(even, 0, rows), jnp.where(even, rows, 0)
    for row in range(rows):
        for field in range(2):
            put_row(lay, window, field, at_own + row, strip[field, row])
            put_row(lay, window, field, at_partner + row, message_row(lay, partner, rows, field, row))
        taps[at_own + row] = own_taps(lay, filters, row)
        taps[at_partner + row] = message_taps(lay, partner, rows, row)
    keep_west, keep_east = keep_lanes(lay)
    at_mine = pl.multiple_of(my_basis() * TAP_ROWS, TAP_ROWS)
    for row in range(2 * rows):
        lines = taps[row, pl.ds(at_mine, TAP_ROWS), :LANES]
        low, high = max(0, row - reach), min(2 * rows, row + reach + 1)
        bands = [
            strip_band(lay, lines[e : e + 1], keep_west, keep_east)
            for e in range(low - row + reach, high - row + reach)
        ]
        source = window[0, low:high].reshape((high - low) * LANES, lay.channels)
        result = product(jnp.concatenate(bands, axis=1), source, ((1,), (0,)))
        basis_out[row * lay.strip : (row + 1) * lay.strip] = result.astype(jnp.bfloat16)
    cot = window[1, :, : lay.strip].reshape(2 * rows * lay.strip, lay.channels)
    grad[...] = (product(basis_out[...], cot, ((0,), (0,))) * scale).astype(jnp.bfloat16)


def across(lay, scale, window, taps, basis_out):
    reach = lay.reach
    keep_west, keep_east = keep_lanes(lay)
    at_mine = pl.multiple_of(my_basis() * TAP_ROWS, TAP_ROWS)
    nothing = jnp.zeros((lay.strip, LANES), jnp.bfloat16)
    for side in range(2):
        rows_of_bands = []
        for row in range(side * reach, (side + 1) * reach):
            lines = taps[row, pl.ds(at_mine, TAP_ROWS), :LANES]
            blocks = []
            for other in range((1 - side) * reach, (2 - side) * reach):
                e = other - row + reach
                inside = 0 <= e < lay.taps
                blocks.append(
                    strip_band(lay, lines[e : e + 1], keep_west, keep_east) if inside else nothing
                )
            rows_of_bands.append(jnp.concatenate(blocks, axis=1))
        source = window[0, (1 - side) * reach : (2 - side) * reach]
        result = product(
            jnp.concatenate(rows_of_bands, axis=0),
            source.reshape(reach * LANES, lay.channels),
            ((1,), (0,)),
        )
        start = side * reach * lay.strip
        basis_out[start : start + reach * lay.strip] = result.astype(jnp.bfloat16)
    cot = window[1, :, : lay.strip].reshape(2 * reach * lay.strip, lay.channels)
    return product(basis_out[...], cot, ((0,), (0,))) * scale


def outer_kernel(lay, scale, strip, filters, outer, inner, grad, window, taps, basis_out):
    rows, reach = lay.rows, lay.reach
    even = lax.axis_index("lat") % 2 == 0
    at_outer, at_own = jnp.where(even, 0, reach), jnp.where(even, reach, 0)
    first = jnp.where(even, 0, rows - reach)
    for row in range(reach):
        for field in range(2):
            put_row(lay, window, field, at_own + row, strip[field, first + row])
            put_row(lay, window, field, at_outer + row, message_row(lay, outer, reach, field, row))
        taps[at_outer + row] = message_taps(lay, outer, reach, row)
        taps[at_own + row] = jnp.where(
            even, own_taps(lay, filters, row), own_taps(lay, filters, rows - reach + row)
        )
    total = inner[...].astype(jnp.float32) + across(lay, scale, window, taps, basis_out)
    grad[...] = total.astype(jnp.bfloat16)


def middle_kernel(lay, scale, near, far, grad, window, taps, basis_out):
    reach = lay.reach
    upper = (lax.axis_index("lat") // 2) % 2 == 0
    at_near, at_far = jnp.where(upper, 0, reach), jnp.where(upper, reach, 0)
    for at, message in ((at_near, near), (at_far, far)):
        for row in range(reach):
            for field in range(2):
                put_row(lay, window, field, at + row, message_row(lay, message, reach, field, row))
            taps[at + row] = message_taps(lay, message, reach, row)
    grad[...] = across(lay, scale, window, taps, basis_out)


def field_kernel(lay, strip, filters, partner, outer, weight, output, field_grad, window, taps, mixed):
    rows, reach, width, basis = lay.rows, lay.reach, lay.width, lay.basis
    even = lax.axis_index("lat") % 2 == 0
    at_outer, at_partner = jnp.where(even, 0, rows + reach), jnp.where(even, rows + reach, 0)
    for field in range(2):
        for row in range(rows):
            put_row(lay, window, field, reach + row, strip[field, row])
        for row in range(reach):
            near = jnp.where(
                even,
                message_row(lay, partner, rows, field, row),
                message_row(lay, partner, rows, field, rows - reach + row),
            )
            put_row(lay, window, field, at_partner + row, near)
            put_row(lay, window, field, at_outer + row, message_row(lay, outer, reach, field, row))
    for row in range(rows):
        taps[reach + row] = own_taps(lay, filters, row)
    for row in range(reach):
        taps[at_partner + row] = jnp.where(
            even,
            message_taps(lay, partner, rows, row),
            message_taps(lay, partner, rows, rows - reach + row),
        )
        taps[at_outer + row] = message_taps(lay, outer, reach, row)

    def bands(row, turned):
        blocks = []
        for n in range(lay.taps):
            at, e = (row + n, lay.taps - 1 - n) if turned else (reach + row, n)
            lanes = slice(LANES, 2 * LANES) if turned else slice(0, LANES)
            parts = []
            for k in range(basis):
                line = taps[at, k * TAP_ROWS + e : k * TAP_ROWS + e + 1, lanes]
                spread = jnp.broadcast_to(line, (width, LANES))
                parts.append(pltpu.roll(spread, int(turned), 1, stride=1, stride_axis=0))
            blocks.append(jnp.concatenate(parts, axis=0).astype(jnp.bfloat16))
        return jnp.concatenate(blocks, axis=1)

    for field, turned, out in ((0, False, output), (1, True, field_grad)):
        for row in range(rows):
            source = window[field, row : row + lay.taps].reshape(lay.taps * LANES, lay.channels)
            result = product(bands(row, turned), source, ((1,), (0,))).astype(jnp.bfloat16)
            for k in range(basis):
                mixed[k, row * width : (row + 1) * width] = result[k * width : (k + 1) * width]
        total = jnp.zeros((rows * width, lay.channels), jnp.float32)
        for k in range(basis):
            total += product(mixed[k], weight[k], ((1,), (1 if turned else 0,)))
        out[...] = total.astype(jnp.bfloat16).reshape(out.shape)


def call(kernel, outs, scratch, flops, name):
    vmem = pl.BlockSpec(memory_space=pltpu.VMEM)

    def run(*operands):
        return pl.pallas_call(
            kernel,
            out_shape=outs,
            in_specs=[vmem] * len(operands),
            out_specs=[vmem] * len(outs),
            scratch_shapes=scratch,
            compiler_params=pltpu.CompilerParams(vmem_limit_bytes=32 * 1024 * 1024),
            cost_estimate=pl.CostEstimate(flops=flops, bytes_accessed=1_000_000, transcendentals=0),
            name=name,
        )(*operands)

    return run


def per_device(features, cotangent, weight, filter_taps, lat_ext, lon_count):
    rows, width, channels = features.shape
    basis = weight.shape[0]
    lat_taps = filter_taps.shape[2]
    lay = Layout(rows, lat_taps // 2, width, basis, channels)
    lat, lon = lax.axis_index("lat"), lax.axis_index("lon")
    even = lat % 2 == 0

    own = jnp.concatenate([features, cotangent], axis=0)
    west = shift(own, "lon", 1)
    own, lat_ext = lax.optimization_barrier((own, lat_ext))
    east = shift(own, "lon", -1)
    support_size = ((2 * lat_ext - 1) * (2 * lon_count - 1)).astype(jnp.float32)
    row_scale = lax.rsqrt(support_size)
    filters = make_filters(filter_taps, lat_ext, lon_count, row_scale)
    gap = jnp.zeros(filters.shape[:-1] + (LANES - filters.shape[-1],), filters.dtype)
    filters = jnp.concatenate([filters, gap, filters[..., ::-1], gap], axis=-1)
    filters = jnp.pad(filters, ((0, 0), (0, 0), (0, TAP_ROWS - lat_taps), (0, 0)))
    per_row = basis * TAP_ROWS
    filters = filters.reshape(rows * per_row, 2 * LANES)

    strip = jnp.concatenate([west, own, east], axis=1).reshape(2, rows, lay.strip, channels)

    partner = flip(jnp.concatenate([strip.reshape(-1, channels), filters], axis=0), "lat", 1)

    def edge(cells, taps, bottom):
        start = jnp.where(bottom, rows - lay.reach, 0)
        cells = lax.dynamic_slice_in_dim(cells.reshape(strip.shape), start, lay.reach, 1)
        taps = lax.dynamic_slice_in_dim(taps, start * per_row, lay.reach * per_row, 0)
        return jnp.concatenate([cells.reshape(-1, channels), taps], axis=0)

    upper = (lat // 2) % 2 == 0
    beside = (lat % 2 == 1) == upper
    near = jnp.where(
        beside, edge(strip, filters, upper), edge(partner[: lay.cells], partner[lay.cells :], upper)
    )
    far = flip(near, "lat", 2)

    def scratch(window_rows, basis_rows):
        return [
            pltpu.VMEM((2, window_rows, LANES, channels), jnp.bfloat16),
            pltpu.VMEM((window_rows, per_row, 2 * LANES), jnp.float32),
            pltpu.VMEM((basis_rows, channels), jnp.bfloat16),
        ]

    scale = 1.0 / math.sqrt(rows * lax.axis_size("lat") * width * lax.axis_size("lon"))
    share = jax.ShapeDtypeStruct((channels, channels), jnp.bfloat16)
    edges = scratch(2 * lay.reach, 2 * lay.reach * lay.strip)
    (grad,) = call(
        functools.partial(inner_kernel, lay, scale),
        [share],
        scratch(2 * rows, 2 * rows * lay.strip),
        INNER_FLOPS,
        "weight_inner",
    )(strip, filters, partner)
    outer = jnp.zeros_like(far)
    if lax.axis_size("lat") > 4:
        outer = outer_swap(edge(strip, filters, jnp.logical_not(even)), "lat")
        outer = jnp.where(beside, jnp.zeros_like(outer), outer)
        (grad,) = call(functools.partial(outer_kernel, lay, scale), [share], edges, MIDDLE_FLOPS, "weight_outer")(
            strip, filters, outer, grad
        )
    got = flip(grad, "lat", 2)
    (middle,) = call(
        functools.partial(middle_kernel, lay, scale),
        [jax.ShapeDtypeStruct((channels, channels), jnp.float32)],
        edges,
        MIDDLE_FLOPS,
        "weight_middle",
    )(near, far)
    grad = (grad.astype(jnp.float32) + got.astype(jnp.float32) + middle).astype(jnp.bfloat16)
    outer = jnp.where(beside, far, outer)
    output, field_grad = call(
        functools.partial(field_kernel, lay),
        [jax.ShapeDtypeStruct(features.shape, jnp.bfloat16)] * 2,
        scratch(rows + 2 * lay.reach, 0)[:2]
        + [pltpu.VMEM((basis, rows * width, channels), jnp.bfloat16)],
        400_000_000,
        "fields",
    )(strip, filters, partner, outer, weight)

    others = [("lat", 1 << b) for b in range(2, lax.axis_size("lat").bit_length() - 1)]
    others += [("lon", 1 << b) for b in range(1, lax.axis_size("lon").bit_length() - 1)]
    for step, (axis, bit) in enumerate(others):
        if step == 1:
            grad, output, field_grad = lax.optimization_barrier((grad, output, field_grad))
        total = grad.astype(jnp.float32) + flip(grad, axis, bit).astype(jnp.float32)
        grad = total.astype(jnp.bfloat16)
    for axis, index in (("lon", lon), ("lat", lat)):
        got = flip(grad, axis, 1)
        upper = index % 2 == 1
        grad = jnp.concatenate([jnp.where(upper, got, grad), jnp.where(upper, grad, got)], axis=0)
    weight_grad = grad.astype(jnp.float32).reshape(basis, channels, channels)
    return (output, field_grad, weight_grad)


def solution(mesh):
    in_specs = (
        P("lat", "lon", None),
        P("lat", "lon", None),
        P(),
        P("lat", None, None, None),
        P("lat"),
        P("lat"),
    )
    out_specs = (P("lat", "lon", None), P("lat", "lon", None), P())
    return jax.shard_map(
        per_device, mesh=mesh, in_specs=in_specs, out_specs=out_specs, check_vma=False
    )
```

```python
import functools
import math

import jax
import jax.numpy as jnp
from jax import lax
from jax.experimental import pallas as pl
from jax.experimental.pallas import tpu as pltpu
from jax.sharding import PartitionSpec as P

LANES = 128
TAP_ROWS = 8
INNER_FLOPS = 300_000_000
MIDDLE_FLOPS = 100_000_000
FIELD_FLOPS = 400_000_000


def shift(block, axis, by):
    count = lax.axis_size(axis)
    return lax.ppermute(block, axis, [(i, (i + by) % count) for i in range(count)])


def flip(block, axis, bit):
    count = lax.axis_size(axis)
    return lax.ppermute(block, axis, [(i, i ^ bit) for i in range(count)])


def outer_swap(block, axis):
    pairs = [(i, i + 1) for i in range(3, lax.axis_size(axis) - 1, 4)]
    return lax.ppermute(block, axis, pairs + [(b, a) for a, b in pairs])


def make_filters(filter_taps, lat_ext, lon_count):
    lat_reach = filter_taps.shape[2] // 2
    half_width = filter_taps.shape[3] // 2
    lat_dist = jnp.abs(jnp.arange(filter_taps.shape[2], dtype=jnp.int32) - lat_reach)
    lon_dist = jnp.abs(jnp.arange(filter_taps.shape[3], dtype=jnp.int32) - half_width)
    support = (lat_dist[None, :, None] < lat_ext[:, None, None]) & (
        lon_dist[None, None, :] < lon_count[:, None, None]
    )
    support_size = ((2 * lat_ext - 1) * (2 * lon_count - 1)).astype(jnp.float32)
    row_scale = lax.rsqrt(support_size)
    masked = (
        filter_taps.astype(jnp.float32)
        * support[:, None].astype(jnp.float32)
        * row_scale[:, None, None, None]
    )
    return masked.astype(jnp.bfloat16)


class Layout:
    def __init__(self, rows, reach, width, basis, channels):
        self.rows, self.reach, self.width = rows, reach, width
        self.basis, self.channels = basis, channels
        self.taps = 2 * reach + 1
        self.strip = 3 * width
        self.cells = 2 * rows * self.strip
        self.side = reach * self.strip


def put_row(lay, window, field, at, cells):
    window[field, at, : lay.strip] = cells
    window[field, at, lay.strip :] = jnp.zeros((LANES - lay.strip, lay.channels), jnp.bfloat16)


def tile(message, start, row):
    return message[start + row * TAP_ROWS : start + (row + 1) * TAP_ROWS]


def put_taps(taps, at, count, message, start):
    for row in range(0, count, 2):
        both = message[start + row * TAP_ROWS : start + (row + 2) * TAP_ROWS].astype(jnp.float32)
        taps[at + row] = both[:TAP_ROWS]
        taps[at + row + 1] = both[TAP_ROWS:]


def lines(lay, rows_taps, block):
    width = 2 * lay.width
    lanes = rows_taps.shape[1]
    moved = pltpu.roll(rows_taps, lax.rem(lanes - block * width, lanes), 1)[:, :LANES]
    lane = lax.broadcasted_iota(jnp.int32, (1, LANES), 1)
    return jnp.where(lane < width, moved, 0.0)


def my_basis():
    return (lax.axis_index("lat") % 2) * 2 + lax.axis_index("lon") % 2


def strip_band(lay, line, keep_west, keep_east):
    width = lay.width
    middle = pltpu.roll(jnp.broadcast_to(line, (width, LANES)), 0, 1, stride=1, stride_axis=0)
    west = pltpu.roll(middle, LANES - width, 1) * keep_west
    east = pltpu.roll(middle, width, 1) * keep_east
    return jnp.concatenate([west, middle, east], axis=0).astype(jnp.bfloat16)


def keep_lanes(lay):
    even = lax.axis_index("lon") % 2 == 0
    lane = lax.broadcasted_iota(jnp.int32, (1, LANES), 1)
    west = jnp.where((lane < lay.width) & even, 0.0, 1.0)
    east = jnp.where((lane >= 2 * lay.width) & jnp.logical_not(even), 0.0, 1.0)
    return west, east


def product(left, right, dims):
    return lax.dot_general(left, right, (dims, ((), ())), preferred_element_type=jnp.float32)


def inner_kernel(lay, scale, strip, filters, partner, grad, window, taps, basis_out):
    rows, reach = lay.rows, lay.reach
    even = lax.axis_index("lat") % 2 == 0
    at_own, at_partner = jnp.where(even, 0, rows), jnp.where(even, rows, 0)
    for row in range(rows):
        for field in range(2):
            start = (field * rows + row) * lay.strip
            put_row(lay, window, field, at_own + row, strip[field, row])
            put_row(lay, window, field, at_partner + row, partner[start : start + lay.strip])
    put_taps(taps, at_own, rows, filters, 0)
    put_taps(taps, at_partner, rows, partner, lay.cells)
    keep_west, keep_east = keep_lanes(lay)
    mine = my_basis()
    for row in range(2 * rows):
        line = lines(lay, taps[row], mine)
        low, high = max(0, row - reach), min(2 * rows, row + reach + 1)
        bands = [
            strip_band(lay, line[e : e + 1], keep_west, keep_east)
            for e in range(low - row + reach, high - row + reach)
        ]
        source = window[0, low:high].reshape((high - low) * LANES, lay.channels)
        result = product(jnp.concatenate(bands, axis=1), source, ((1,), (0,)))
        basis_out[row * lay.strip : (row + 1) * lay.strip] = result.astype(jnp.bfloat16)
    cot = window[1, :, : lay.strip].reshape(2 * rows * lay.strip, lay.channels)
    grad[...] = (product(basis_out[...], cot, ((0,), (0,))) * scale).astype(jnp.bfloat16)


def across(lay, scale, window, taps, basis_out):
    reach = lay.reach
    keep_west, keep_east = keep_lanes(lay)
    mine = my_basis()
    nothing = jnp.zeros((lay.strip, LANES), jnp.bfloat16)
    for side in range(2):
        rows_of_bands = []
        for row in range(side * reach, (side + 1) * reach):
            line = lines(lay, taps[row], mine)
            blocks = []
            for other in range((1 - side) * reach, (2 - side) * reach):
                e = other - row + reach
                inside = 0 <= e < lay.taps
                blocks.append(strip_band(lay, line[e : e + 1], keep_west, keep_east) if inside else nothing)
            rows_of_bands.append(jnp.concatenate(blocks, axis=1))
        source = window[0, (1 - side) * reach : (2 - side) * reach]
        result = product(
            jnp.concatenate(rows_of_bands, axis=0),
            source.reshape(reach * LANES, lay.channels),
            ((1,), (0,)),
        )
        basis_out[side * lay.side : (side + 1) * lay.side] = result.astype(jnp.bfloat16)
    cot = window[1, :, : lay.strip].reshape(2 * lay.side, lay.channels)
    return product(basis_out[...], cot, ((0,), (0,))) * scale


def outer_kernel(lay, scale, near, outer, inner, grad, window, taps, basis_out):
    reach = lay.reach
    even = lax.axis_index("lat") % 2 == 0
    at_outer, at_near = jnp.where(even, 0, reach), jnp.where(even, reach, 0)
    for at, message in ((at_near, near), (at_outer, outer)):
        for row in range(reach):
            for field in range(2):
                start = field * lay.side + row * lay.strip
                put_row(lay, window, field, at + row, message[start : start + lay.strip])
        put_taps(taps, at, reach, message, 2 * lay.side)
    total = inner[...].astype(jnp.float32) + across(lay, scale, window, taps, basis_out)
    grad[...] = total.astype(jnp.bfloat16)


def middle_kernel(lay, scale, near, far, passed, grad, window, taps, basis_out):
    reach = lay.reach
    lat = lax.axis_index("lat")
    upper = (lat // 2) % 2 == 0
    first = lat % 2 == 0
    at_near, at_far = jnp.where(upper, 0, reach), jnp.where(upper, reach, 0)
    for row in range(reach):
        cells = slice(row * lay.strip, (row + 1) * lay.strip)
        put_row(lay, window, 0, at_far + row, jnp.where(first, far[cells], passed[cells]))
        put_row(lay, window, 1, at_far + row, jnp.where(first, passed[cells], far[cells]))
        for field in range(2):
            start = field * lay.side + row * lay.strip
            put_row(lay, window, field, at_near + row, near[start : start + lay.strip])
    put_taps(taps, at_near, reach, near, 2 * lay.side)
    put_taps(taps, at_far, reach, far, lay.side)
    grad[...] = across(lay, scale, window, taps, basis_out)


def field_kernel(
    lay, strip, filters, partner, outer, turned, turned_partner, turned_outer, weight,
    output, field_grad, window, taps, mixed,
):
    rows, reach, width, basis = lay.rows, lay.reach, lay.width, lay.basis
    even = lax.axis_index("lat") % 2 == 0
    at_outer, at_partner = jnp.where(even, 0, rows + reach), jnp.where(even, rows + reach, 0)
    for field in range(2):
        for row in range(rows):
            put_row(lay, window, field, reach + row, strip[field, row])
        for row in range(reach):
            start = (field * rows + row) * lay.strip
            last = start + (rows - reach) * lay.strip
            near = jnp.where(even, partner[start : start + lay.strip], partner[last : last + lay.strip])
            put_row(lay, window, field, at_partner + row, near)
            start = field * lay.side + row * lay.strip
            put_row(lay, window, field, at_outer + row, outer[start : start + lay.strip])

    def bands(row, is_turned):
        blocks = []
        for n in range(lay.taps):
            at, e = (row + n, lay.taps - 1 - n) if is_turned else (reach + row, n)
            parts = []
            for k in range(basis):
                spread = jnp.broadcast_to(taps[at, k, e : e + 1], (width, LANES))
                parts.append(pltpu.roll(spread, int(is_turned), 1, stride=1, stride_axis=0))
            blocks.append(jnp.concatenate(parts, axis=0).astype(jnp.bfloat16))
        return jnp.concatenate(blocks, axis=1)

    def put(at, message, start, count, is_turned):
        both = message[start : start + count * TAP_ROWS].astype(jnp.float32)
        for row in range(count):
            for k in range(basis):
                block = basis - 1 - k if is_turned else k
                taps[at + row, k] = lines(lay, both[row * TAP_ROWS : (row + 1) * TAP_ROWS], block)

    for field, is_turned, out in ((0, False, output), (1, True, field_grad)):
        if is_turned:
            put(reach, turned, 0, rows, True)
            put(at_partner, turned_partner, 0, reach, True)
            put(at_outer, turned_outer, 0, reach, True)
        else:
            put(reach, filters, 0, rows, False)
        for row in range(rows):
            source = window[field, row : row + lay.taps].reshape(lay.taps * LANES, lay.channels)
            result = product(bands(row, is_turned), source, ((1,), (0,))).astype(jnp.bfloat16)
            for k in range(basis):
                mixed[k, row * width : (row + 1) * width] = result[k * width : (k + 1) * width]
        total = jnp.zeros((rows * width, lay.channels), jnp.float32)
        for k in range(basis):
            total += product(mixed[k], weight[k], ((1,), (1 if is_turned else 0,)))
        out[...] = total.astype(jnp.bfloat16).reshape(out.shape)


def call(kernel, outs, scratch, flops, name):
    vmem = pl.BlockSpec(memory_space=pltpu.VMEM)

    def run(*operands):
        return pl.pallas_call(
            kernel,
            out_shape=outs,
            in_specs=[vmem] * len(operands),
            out_specs=[vmem] * len(outs),
            scratch_shapes=scratch,
            compiler_params=pltpu.CompilerParams(vmem_limit_bytes=32 * 1024 * 1024),
            cost_estimate=pl.CostEstimate(flops=flops, bytes_accessed=1_000_000, transcendentals=0),
            name=name,
        )(*operands)

    return run


def per_device(features, cotangent, weight, filter_taps, lat_ext, lon_count):
    rows, width, channels = features.shape
    basis = weight.shape[0]
    lat_taps = filter_taps.shape[2]
    lay = Layout(rows, lat_taps // 2, width, basis, channels)
    reach = lay.reach
    lat, lon = lax.axis_index("lat"), lax.axis_index("lon")
    even = lat % 2 == 0

    own = jnp.concatenate([features, cotangent], axis=0)
    west = shift(own, "lon", 1)
    own, lat_ext = lax.optimization_barrier((own, lat_ext))
    east = shift(own, "lon", -1)
    filters = make_filters(filter_taps, lat_ext, lon_count)
    filters = jnp.pad(jnp.swapaxes(filters, 1, 2), ((0, 0), (0, TAP_ROWS - lat_taps), (0, 0), (0, 0)))
    filters = filters.reshape(rows * TAP_ROWS, channels)

    strip = jnp.concatenate([west, own, east], axis=1).reshape(2, rows, lay.strip, channels)
    partner = flip(jnp.concatenate([strip.reshape(-1, channels), filters], axis=0), "lat", 1)
    partner_taps = partner[lay.cells :]

    def edge(cells, taps, bottom):
        start = jnp.where(bottom, rows - reach, 0)
        cells = lax.dynamic_slice_in_dim(cells.reshape(strip.shape), start, reach, 1)
        taps = lax.dynamic_slice_in_dim(taps, start * TAP_ROWS, reach * TAP_ROWS, 0)
        return jnp.concatenate([cells.reshape(-1, channels), taps], axis=0)

    upper = (lat // 2) % 2 == 0
    beside = (lat % 2 == 1) == upper
    near = jnp.where(beside, edge(strip, filters, upper), edge(partner[: lay.cells], partner_taps, upper))
    piece = lax.dynamic_slice_in_dim(near, (lat % 2) * lay.side, lay.side, 0)
    far = flip(jnp.concatenate([piece, near[2 * lay.side :]], axis=0), "lat", 2)

    def scratch(window_rows, basis_rows):
        return [
            pltpu.VMEM((2, window_rows, LANES, channels), jnp.bfloat16),
            pltpu.VMEM((window_rows, TAP_ROWS, channels), jnp.float32),
            pltpu.VMEM((basis_rows, channels), jnp.bfloat16),
        ]

    scale = 1.0 / math.sqrt(rows * lax.axis_size("lat") * width * lax.axis_size("lon"))
    share = jax.ShapeDtypeStruct((channels, channels), jnp.bfloat16)
    edges = scratch(2 * reach, 2 * lay.side)
    (grad,) = call(
        functools.partial(inner_kernel, lay, scale),
        [share],
        scratch(2 * rows, 2 * rows * lay.strip),
        INNER_FLOPS,
        "weight_inner",
    )(strip, filters, partner)
    outer = None
    if lax.axis_size("lat") > 4:
        bottom = jnp.logical_not(even)
        outward = edge(strip, filters, bottom)
        outer = outer_swap(outward, "lat")
        (grad,) = call(functools.partial(outer_kernel, lay, scale), [share], edges, MIDDLE_FLOPS, "weight_outer")(
            outward, outer, grad
        )
    got = flip(grad, "lat", 2)
    far, grad = lax.optimization_barrier((far, grad))
    passed = flip(far[: lay.side], "lat", 1)
    (middle,) = call(
        functools.partial(middle_kernel, lay, scale),
        [jax.ShapeDtypeStruct((channels, channels), jnp.float32)],
        edges,
        MIDDLE_FLOPS,
        "weight_middle",
    )(near, far, passed)
    grad = (grad.astype(jnp.float32) + got.astype(jnp.float32) + middle).astype(jnp.bfloat16)

    beyond = jnp.concatenate(
        [jnp.where(even, far[: lay.side], passed), jnp.where(even, passed, far[: lay.side]), far[lay.side :]], axis=0
    )
    outer = jnp.where(beside, beyond, jnp.zeros_like(beyond) if outer is None else outer)
    output, field_grad = call(
        functools.partial(field_kernel, lay),
        [jax.ShapeDtypeStruct(features.shape, jnp.bfloat16)] * 2,
        [
            pltpu.VMEM((2, rows + 2 * reach, LANES, channels), jnp.bfloat16),
            pltpu.VMEM((rows + 2 * reach, basis, TAP_ROWS, LANES), jnp.float32),
            pltpu.VMEM((basis, rows * width, channels), jnp.bfloat16),
        ],
        FIELD_FLOPS,
        "fields",
    )(
        strip,
        filters,
        partner,
        outer,
        filters[:, ::-1],
        edge(partner[: lay.cells], partner_taps, jnp.logical_not(even))[2 * lay.side :, ::-1],
        outer[2 * lay.side :, ::-1],
        weight,
    )

    others = [("lat", 1 << b) for b in range(2, lax.axis_size("lat").bit_length() - 1)]
    others += [("lon", 1 << b) for b in range(1, lax.axis_size("lon").bit_length() - 1)]
    for step, (axis, bit) in enumerate(others):
        if step == 1:
            grad, output, field_grad = lax.optimization_barrier((grad, output, field_grad))
        total = grad.astype(jnp.float32) + flip(grad, axis, bit).astype(jnp.float32)
        grad = total.astype(jnp.bfloat16)
    for axis, index in (("lon", lon), ("lat", lat)):
        got = flip(grad, axis, 1)
        second = index % 2 == 1
        grad = jnp.concatenate([jnp.where(second, got, grad), jnp.where(second, grad, got)], axis=0)
    weight_grad = grad.astype(jnp.float32).reshape(basis, channels, channels)
    return (output, field_grad, weight_grad)


def solution(mesh):
    in_specs = (
        P("lat", "lon", None),
        P("lat", "lon", None),
        P(),
        P("lat", None, None, None),
        P("lat"),
        P("lat"),
    )
    out_specs = (P("lat", "lon", None), P("lat", "lon", None), P())
    return jax.shard_map(
        per_device, mesh=mesh, in_specs=in_specs, out_specs=out_specs, check_vma=False
    )
```

```python
import functools
import math

import jax
import jax.numpy as jnp
from jax import lax
from jax.experimental import pallas as pl
from jax.experimental.pallas import tpu as pltpu
from jax.sharding import PartitionSpec as P

LANES = 128
TAP_ROWS = 8
INNER_FLOPS = 300_000_000
MIDDLE_FLOPS = 100_000_000
FIELD_FLOPS = 400_000_000


def shift(block, axis, by):
    count = lax.axis_size(axis)
    return lax.ppermute(block, axis, [(i, (i + by) % count) for i in range(count)])


def flip(block, axis, bit):
    count = lax.axis_size(axis)
    return lax.ppermute(block, axis, [(i, i ^ bit) for i in range(count)])


def outer_swap(block, axis):
    pairs = [(i, i + 1) for i in range(3, lax.axis_size(axis) - 1, 4)]
    return lax.ppermute(block, axis, pairs + [(b, a) for a, b in pairs])


def make_filters(filter_taps, lat_ext, lon_count):
    lat_reach = filter_taps.shape[2] // 2
    half_width = filter_taps.shape[3] // 2
    lat_dist = jnp.abs(jnp.arange(filter_taps.shape[2], dtype=jnp.int32) - lat_reach)
    lon_dist = jnp.abs(jnp.arange(filter_taps.shape[3], dtype=jnp.int32) - half_width)
    support = (lat_dist[None, :, None] < lat_ext[:, None, None]) & (
        lon_dist[None, None, :] < lon_count[:, None, None]
    )
    support_size = ((2 * lat_ext - 1) * (2 * lon_count - 1)).astype(jnp.float32)
    row_scale = lax.rsqrt(support_size)
    masked = (
        filter_taps.astype(jnp.float32)
        * support[:, None].astype(jnp.float32)
        * row_scale[:, None, None, None]
    )
    return masked.astype(jnp.bfloat16)


class Layout:
    def __init__(self, rows, reach, width, basis, channels):
        self.rows, self.reach, self.width = rows, reach, width
        self.basis, self.channels = basis, channels
        self.taps = 2 * reach + 1
        self.strip = 3 * width
        self.cells = 2 * rows * self.strip
        self.side = reach * self.strip


def put_row(lay, window, field, at, cells):
    window[field, at, : lay.strip] = cells
    window[field, at, lay.strip :] = jnp.zeros((LANES - lay.strip, lay.channels), jnp.bfloat16)


def tile(message, start, row):
    return message[start + row * TAP_ROWS : start + (row + 1) * TAP_ROWS]


def put_taps(taps, at, count, message, start):
    for row in range(0, count, 2):
        both = message[start + row * TAP_ROWS : start + (row + 2) * TAP_ROWS].astype(jnp.float32)
        taps[at + row] = both[:TAP_ROWS]
        taps[at + row + 1] = both[TAP_ROWS:]


def lines(lay, rows_taps, block):
    width = 2 * lay.width
    lanes = rows_taps.shape[1]
    moved = pltpu.roll(rows_taps, lax.rem(lanes - block * width, lanes), 1)[:, :LANES]
    lane = lax.broadcasted_iota(jnp.int32, (1, LANES), 1)
    return jnp.where(lane < width, moved, 0.0)


def my_basis():
    return (lax.axis_index("lat") % 2) * 2 + lax.axis_index("lon") % 2


def strip_band(lay, line, keep_west, keep_east):
    width = lay.width
    middle = pltpu.roll(jnp.broadcast_to(line, (width, LANES)), 0, 1, stride=1, stride_axis=0)
    west = pltpu.roll(middle, LANES - width, 1) * keep_west
    east = pltpu.roll(middle, width, 1) * keep_east
    return jnp.concatenate([west, middle, east], axis=0).astype(jnp.bfloat16)


def keep_lanes(lay):
    even = lax.axis_index("lon") % 2 == 0
    lane = lax.broadcasted_iota(jnp.int32, (1, LANES), 1)
    west = jnp.where((lane < lay.width) & even, 0.0, 1.0)
    east = jnp.where((lane >= 2 * lay.width) & jnp.logical_not(even), 0.0, 1.0)
    return west, east


def product(left, right, dims):
    return lax.dot_general(left, right, (dims, ((), ())), preferred_element_type=jnp.float32)


def inner_kernel(lay, scale, strip, filters, partner, grad, window, taps, basis_out):
    rows, reach = lay.rows, lay.reach
    even = lax.axis_index("lat") % 2 == 0
    at_own, at_partner = jnp.where(even, 0, rows), jnp.where(even, rows, 0)
    for row in range(rows):
        for field in range(2):
            start = (field * rows + row) * lay.strip
            put_row(lay, window, field, at_own + row, strip[field, row])
            put_row(lay, window, field, at_partner + row, partner[start : start + lay.strip])
    put_taps(taps, at_own, rows, filters, 0)
    put_taps(taps, at_partner, rows, partner, lay.cells)
    keep_west, keep_east = keep_lanes(lay)
    mine = my_basis()
    for row in range(2 * rows):
        line = lines(lay, taps[row], mine)
        low, high = max(0, row - reach), min(2 * rows, row + reach + 1)
        bands = [
            strip_band(lay, line[e : e + 1], keep_west, keep_east)
            for e in range(low - row + reach, high - row + reach)
        ]
        source = window[0, low:high].reshape((high - low) * LANES, lay.channels)
        result = product(jnp.concatenate(bands, axis=1), source, ((1,), (0,)))
        basis_out[row * lay.strip : (row + 1) * lay.strip] = result.astype(jnp.bfloat16)
    cot = window[1, :, : lay.strip].reshape(2 * rows * lay.strip, lay.channels)
    grad[...] = (product(basis_out[...], cot, ((0,), (0,))) * scale).astype(jnp.bfloat16)


def across(lay, scale, window, taps, basis_out):
    reach = lay.reach
    keep_west, keep_east = keep_lanes(lay)
    mine = my_basis()
    nothing = jnp.zeros((lay.strip, LANES), jnp.bfloat16)
    for side in range(2):
        rows_of_bands = []
        for row in range(side * reach, (side + 1) * reach):
            line = lines(lay, taps[row], mine)
            blocks = []
            for other in range((1 - side) * reach, (2 - side) * reach):
                e = other - row + reach
                inside = 0 <= e < lay.taps
                blocks.append(strip_band(lay, line[e : e + 1], keep_west, keep_east) if inside else nothing)
            rows_of_bands.append(jnp.concatenate(blocks, axis=1))
        source = window[0, (1 - side) * reach : (2 - side) * reach]
        result = product(
            jnp.concatenate(rows_of_bands, axis=0),
            source.reshape(reach * LANES, lay.channels),
            ((1,), (0,)),
        )
        basis_out[side * lay.side : (side + 1) * lay.side] = result.astype(jnp.bfloat16)
    cot = window[1, :, : lay.strip].reshape(2 * lay.side, lay.channels)
    return product(basis_out[...], cot, ((0,), (0,))) * scale


def outer_kernel(lay, scale, near, outer, inner, grad, window, taps, basis_out):
    reach = lay.reach
    even = lax.axis_index("lat") % 2 == 0
    at_outer, at_near = jnp.where(even, 0, reach), jnp.where(even, reach, 0)
    for at, message in ((at_near, near), (at_outer, outer)):
        for row in range(reach):
            for field in range(2):
                start = field * lay.side + row * lay.strip
                put_row(lay, window, field, at + row, message[start : start + lay.strip])
        put_taps(taps, at, reach, message, 2 * lay.side)
    total = inner[...].astype(jnp.float32) + across(lay, scale, window, taps, basis_out)
    grad[...] = total.astype(jnp.bfloat16)


def middle_kernel(lay, scale, near, far, passed, grad, window, taps, basis_out):
    reach = lay.reach
    lat = lax.axis_index("lat")
    upper = (lat // 2) % 2 == 0
    first = lat % 2 == 0
    at_near, at_far = jnp.where(upper, 0, reach), jnp.where(upper, reach, 0)
    for row in range(reach):
        cells = slice(row * lay.strip, (row + 1) * lay.strip)
        put_row(lay, window, 0, at_far + row, jnp.where(first, far[cells], passed[cells]))
        put_row(lay, window, 1, at_far + row, jnp.where(first, passed[cells], far[cells]))
        for field in range(2):
            start = field * lay.side + row * lay.strip
            put_row(lay, window, field, at_near + row, near[start : start + lay.strip])
    put_taps(taps, at_near, reach, near, 2 * lay.side)
    put_taps(taps, at_far, reach, far, lay.side)
    grad[...] = across(lay, scale, window, taps, basis_out)


def field_kernel(
    lay, strip, filters, partner, outer, turned, turned_partner, turned_outer, weight,
    output, field_grad, window, taps, mixed,
):
    rows, reach, width, basis = lay.rows, lay.reach, lay.width, lay.basis
    even = lax.axis_index("lat") % 2 == 0
    at_outer, at_partner = jnp.where(even, 0, rows + reach), jnp.where(even, rows + reach, 0)
    for field in range(2):
        for row in range(rows):
            put_row(lay, window, field, reach + row, strip[field, row])
        for row in range(reach):
            start = (field * rows + row) * lay.strip
            last = start + (rows - reach) * lay.strip
            near = jnp.where(even, partner[start : start + lay.strip], partner[last : last + lay.strip])
            put_row(lay, window, field, at_partner + row, near)
            start = field * lay.side + row * lay.strip
            put_row(lay, window, field, at_outer + row, outer[start : start + lay.strip])

    def bands(row, is_turned):
        blocks = []
        for n in range(lay.taps):
            at, e = (row + n, lay.taps - 1 - n) if is_turned else (reach + row, n)
            parts = []
            for k in range(basis):
                spread = jnp.broadcast_to(taps[at, k, e : e + 1], (width, LANES))
                parts.append(pltpu.roll(spread, int(is_turned), 1, stride=1, stride_axis=0))
            blocks.append(jnp.concatenate(parts, axis=0).astype(jnp.bfloat16))
        return jnp.concatenate(blocks, axis=1)

    def put(at, message, start, count, is_turned):
        both = message[start : start + count * TAP_ROWS].astype(jnp.float32)
        for row in range(count):
            for k in range(basis):
                block = basis - 1 - k if is_turned else k
                taps[at + row, k] = lines(lay, both[row * TAP_ROWS : (row + 1) * TAP_ROWS], block)

    for field, is_turned, out in ((0, False, output), (1, True, field_grad)):
        if is_turned:
            put(reach, turned, 0, rows, True)
            put(at_partner, turned_partner, 0, reach, True)
            put(at_outer, turned_outer, 0, reach, True)
        else:
            put(reach, filters, 0, rows, False)
        for row in range(rows):
            source = window[field, row : row + lay.taps].reshape(lay.taps * LANES, lay.channels)
            result = product(bands(row, is_turned), source, ((1,), (0,))).astype(jnp.bfloat16)
            for k in range(basis):
                mixed[k, row * width : (row + 1) * width] = result[k * width : (k + 1) * width]
        total = jnp.zeros((rows * width, lay.channels), jnp.float32)
        for k in range(basis):
            total += product(mixed[k], weight[k], ((1,), (1 if is_turned else 0,)))
        out[...] = total.astype(jnp.bfloat16).reshape(out.shape)


def call(kernel, outs, scratch, flops, name):
    vmem = pl.BlockSpec(memory_space=pltpu.VMEM)

    def run(*operands):
        return pl.pallas_call(
            kernel,
            out_shape=outs,
            in_specs=[vmem] * len(operands),
            out_specs=[vmem] * len(outs),
            scratch_shapes=scratch,
            compiler_params=pltpu.CompilerParams(vmem_limit_bytes=32 * 1024 * 1024),
            cost_estimate=pl.CostEstimate(flops=flops, bytes_accessed=1_000_000, transcendentals=0),
            name=name,
        )(*operands)

    return run


def per_device(features, cotangent, weight, filter_taps, lat_ext, lon_count):
    rows, width, channels = features.shape
    basis = weight.shape[0]
    lat_taps = filter_taps.shape[2]
    lay = Layout(rows, lat_taps // 2, width, basis, channels)
    reach = lay.reach
    lat, lon = lax.axis_index("lat"), lax.axis_index("lon")
    even = lat % 2 == 0

    own = jnp.concatenate([features, cotangent], axis=0)
    west = shift(own, "lon", 1)
    own, lat_ext = lax.optimization_barrier((own, lat_ext))
    east = shift(own, "lon", -1)
    filters = make_filters(filter_taps, lat_ext, lon_count)
    filters = jnp.pad(jnp.swapaxes(filters, 1, 2), ((0, 0), (0, TAP_ROWS - lat_taps), (0, 0), (0, 0)))
    filters = filters.reshape(rows * TAP_ROWS, channels)

    strip = jnp.concatenate([west, own, east], axis=1).reshape(2, rows, lay.strip, channels)
    partner = flip(jnp.concatenate([strip.reshape(-1, channels), filters], axis=0), "lat", 1)
    partner_taps = partner[lay.cells :]

    def edge(cells, taps, bottom):
        start = jnp.where(bottom, rows - reach, 0)
        cells = lax.dynamic_slice_in_dim(cells.reshape(strip.shape), start, reach, 1)
        taps = lax.dynamic_slice_in_dim(taps, start * TAP_ROWS, reach * TAP_ROWS, 0)
        return jnp.concatenate([cells.reshape(-1, channels), taps], axis=0)

    upper = (lat // 2) % 2 == 0
    beside = (lat % 2 == 1) == upper
    near = jnp.where(beside, edge(strip, filters, upper), edge(partner[: lay.cells], partner_taps, upper))
    piece = lax.dynamic_slice_in_dim(near, (lat % 2) * lay.side, lay.side, 0)
    far = flip(jnp.concatenate([piece, near[2 * lay.side :]], axis=0), "lat", 2)

    def scratch(window_rows, basis_rows):
        return [
            pltpu.VMEM((2, window_rows, LANES, channels), jnp.bfloat16),
            pltpu.VMEM((window_rows, TAP_ROWS, channels), jnp.float32),
            pltpu.VMEM((basis_rows, channels), jnp.bfloat16),
        ]

    scale = 1.0 / math.sqrt(rows * lax.axis_size("lat") * width * lax.axis_size("lon"))
    share = jax.ShapeDtypeStruct((channels, channels), jnp.bfloat16)
    edges = scratch(2 * reach, 2 * lay.side)
    (grad,) = call(
        functools.partial(inner_kernel, lay, scale),
        [share],
        scratch(2 * rows, 2 * rows * lay.strip),
        INNER_FLOPS,
        "weight_inner",
    )(strip, filters, partner)
    outer = None
    if lax.axis_size("lat") > 4:
        bottom = jnp.logical_not(even)
        outward = edge(strip, filters, bottom)
        outer = outer_swap(outward, "lat")
        (grad,) = call(functools.partial(outer_kernel, lay, scale), [share], edges, MIDDLE_FLOPS, "weight_outer")(
            outward, outer, grad
        )
    got = flip(grad, "lat", 2)
    far, grad = lax.optimization_barrier((far, grad))
    passed = flip(far[: lay.side], "lat", 1)
    (middle,) = call(
        functools.partial(middle_kernel, lay, scale),
        [jax.ShapeDtypeStruct((channels, channels), jnp.float32)],
        edges,
        MIDDLE_FLOPS,
        "weight_middle",
    )(near, far, passed)
    grad = (grad.astype(jnp.float32) + got.astype(jnp.float32) + middle).astype(jnp.bfloat16)

    beyond = jnp.concatenate(
        [jnp.where(even, far[: lay.side], passed), jnp.where(even, passed, far[: lay.side]), far[lay.side :]], axis=0
    )
    outer = jnp.where(beside, beyond, jnp.zeros_like(beyond) if outer is None else outer)
    output, field_grad = call(
        functools.partial(field_kernel, lay),
        [jax.ShapeDtypeStruct(features.shape, jnp.bfloat16)] * 2,
        [
            pltpu.VMEM((2, rows + 2 * reach, LANES, channels), jnp.bfloat16),
            pltpu.VMEM((rows + 2 * reach, basis, TAP_ROWS, LANES), jnp.float32),
            pltpu.VMEM((basis, rows * width, channels), jnp.bfloat16),
        ],
        FIELD_FLOPS,
        "fields",
    )(
        strip,
        filters,
        partner,
        outer,
        filters[:, ::-1],
        edge(partner[: lay.cells], partner_taps, jnp.logical_not(even))[2 * lay.side :, ::-1],
        outer[2 * lay.side :, ::-1],
        weight,
    )

    lat_count, lon_count_devices = lax.axis_size("lat"), lax.axis_size("lon")
    lat_bits = [1 << b for b in range(2, lat_count.bit_length() - 1)]
    lon_bits = [1 << b for b in range(1, lon_count_devices.bit_length() - 1)]
    rounds = [(bit, bit, 0, 0) for bit in lat_bits]
    rounds += [(0, 0, up, down) for up, down in zip(lon_bits, lon_bits[::-1], strict=True)]
    for step, (lat_even, lat_odd, lon_even, lon_odd) in enumerate(rounds):
        if step == 1:
            grad, output, field_grad = lax.optimization_barrier((grad, output, field_grad))
        pairs = []
        for a in range(lat_count):
            lat_bit, lon_bit = (lat_odd, lon_odd) if a % 2 else (lat_even, lon_even)
            for o in range(lon_count_devices):
                pairs.append((a * lon_count_devices + o, (a ^ lat_bit) * lon_count_devices + (o ^ lon_bit)))
        got = lax.ppermute(grad, ("lat", "lon"), pairs)
        grad = (grad.astype(jnp.float32) + got.astype(jnp.float32)).astype(jnp.bfloat16)
    for axis, index in (("lon", lon), ("lat", lat)):
        got = flip(grad, axis, 1)
        second = index % 2 == 1
        grad = jnp.concatenate([jnp.where(second, got, grad), jnp.where(second, grad, got)], axis=0)
    weight_grad = grad.astype(jnp.float32).reshape(basis, channels, channels)
    return (output, field_grad, weight_grad)


def solution(mesh):
    in_specs = (
        P("lat", "lon", None),
        P("lat", "lon", None),
        P(),
        P("lat", None, None, None),
        P("lat"),
        P("lat"),
    )
    out_specs = (P("lat", "lon", None), P("lat", "lon", None), P())
    return jax.shard_map(
        per_device, mesh=mesh, in_specs=in_specs, out_specs=out_specs, check_vma=False
    )
```

```python
import functools
import math

import jax
import jax.numpy as jnp
from jax import lax
from jax.experimental import pallas as pl
from jax.experimental.pallas import tpu as pltpu
from jax.sharding import PartitionSpec as P

LANES = 128
TAP_ROWS = 8
INNER_FLOPS = 300_000_000
MIDDLE_FLOPS = 100_000_000
FIELD_FLOPS = 400_000_000


def shift(block, axis, by):
    count = lax.axis_size(axis)
    return lax.ppermute(block, axis, [(i, (i + by) % count) for i in range(count)])


def flip(block, axis, bit):
    count = lax.axis_size(axis)
    return lax.ppermute(block, axis, [(i, i ^ bit) for i in range(count)])


def outer_swap(block, axis):
    pairs = [(i, i + 1) for i in range(3, lax.axis_size(axis) - 1, 4)]
    return lax.ppermute(block, axis, pairs + [(b, a) for a, b in pairs])


def make_filters(filter_taps, lat_ext, lon_count):
    lat_reach = filter_taps.shape[2] // 2
    half_width = filter_taps.shape[3] // 2
    lat_dist = jnp.abs(jnp.arange(filter_taps.shape[2], dtype=jnp.int32) - lat_reach)
    lon_dist = jnp.abs(jnp.arange(filter_taps.shape[3], dtype=jnp.int32) - half_width)
    support = (lat_dist[None, :, None] < lat_ext[:, None, None]) & (
        lon_dist[None, None, :] < lon_count[:, None, None]
    )
    support_size = ((2 * lat_ext - 1) * (2 * lon_count - 1)).astype(jnp.float32)
    row_scale = lax.rsqrt(support_size)
    masked = (
        filter_taps.astype(jnp.float32)
        * support[:, None].astype(jnp.float32)
        * row_scale[:, None, None, None]
    )
    return masked.astype(jnp.bfloat16)


class Layout:
    def __init__(self, rows, reach, width, basis, channels):
        self.rows, self.reach, self.width = rows, reach, width
        self.basis, self.channels = basis, channels
        self.taps = 2 * reach + 1
        self.strip = 3 * width
        self.cells = 2 * rows * self.strip
        self.side = reach * self.strip


def put_row(lay, window, field, at, cells):
    window[field, at, : lay.strip] = cells
    window[field, at, lay.strip :] = jnp.zeros((LANES - lay.strip, lay.channels), jnp.bfloat16)


def tile(message, start, row):
    return message[start + row * TAP_ROWS : start + (row + 1) * TAP_ROWS]


def put_taps(taps, at, count, message, start):
    for row in range(0, count, 2):
        both = message[start + row * TAP_ROWS : start + (row + 2) * TAP_ROWS].astype(jnp.float32)
        taps[at + row] = both[:TAP_ROWS]
        taps[at + row + 1] = both[TAP_ROWS:]


def lines(lay, rows_taps, block):
    width = 2 * lay.width
    lanes = rows_taps.shape[1]
    moved = pltpu.roll(rows_taps, lax.rem(lanes - block * width, lanes), 1)[:, :LANES]
    lane = lax.broadcasted_iota(jnp.int32, (1, LANES), 1)
    return jnp.where(lane < width, moved, 0.0)


def my_basis():
    return (lax.axis_index("lat") % 2) * 2 + lax.axis_index("lon") % 2


def strip_band(lay, line, keep_west, keep_east):
    width = lay.width
    middle = pltpu.roll(jnp.broadcast_to(line, (width, LANES)), 0, 1, stride=1, stride_axis=0)
    west = pltpu.roll(middle, LANES - width, 1) * keep_west
    east = pltpu.roll(middle, width, 1) * keep_east
    return jnp.concatenate([west, middle, east], axis=0).astype(jnp.bfloat16)


def keep_lanes(lay):
    even = lax.axis_index("lon") % 2 == 0
    lane = lax.broadcasted_iota(jnp.int32, (1, LANES), 1)
    west = jnp.where((lane < lay.width) & even, 0.0, 1.0)
    east = jnp.where((lane >= 2 * lay.width) & jnp.logical_not(even), 0.0, 1.0)
    return west, east


def product(left, right, dims):
    return lax.dot_general(left, right, (dims, ((), ())), preferred_element_type=jnp.float32)


def inner_kernel(lay, scale, strip, filters, partner, grad, window, taps, basis_out):
    rows, reach = lay.rows, lay.reach
    even = lax.axis_index("lat") % 2 == 0
    at_own, at_partner = jnp.where(even, 0, rows), jnp.where(even, rows, 0)
    for row in range(rows):
        for field in range(2):
            start = (field * rows + row) * lay.strip
            put_row(lay, window, field, at_own + row, strip[field, row])
            put_row(lay, window, field, at_partner + row, partner[start : start + lay.strip])
    put_taps(taps, at_own, rows, filters, 0)
    put_taps(taps, at_partner, rows, partner, lay.cells)
    keep_west, keep_east = keep_lanes(lay)
    mine = my_basis()
    for row in range(2 * rows):
        line = lines(lay, taps[row], mine)
        low, high = max(0, row - reach), min(2 * rows, row + reach + 1)
        bands = [
            strip_band(lay, line[e : e + 1], keep_west, keep_east)
            for e in range(low - row + reach, high - row + reach)
        ]
        source = window[0, low:high].reshape((high - low) * LANES, lay.channels)
        result = product(jnp.concatenate(bands, axis=1), source, ((1,), (0,)))
        basis_out[row * lay.strip : (row + 1) * lay.strip] = result.astype(jnp.bfloat16)
    cot = window[1, :, : lay.strip].reshape(2 * rows * lay.strip, lay.channels)
    grad[...] = (product(basis_out[...], cot, ((0,), (0,))) * scale).astype(jnp.bfloat16)


def across(lay, scale, window, taps, basis_out):
    reach = lay.reach
    keep_west, keep_east = keep_lanes(lay)
    mine = my_basis()
    nothing = jnp.zeros((lay.strip, LANES), jnp.bfloat16)
    for side in range(2):
        rows_of_bands = []
        for row in range(side * reach, (side + 1) * reach):
            line = lines(lay, taps[row], mine)
            blocks = []
            for other in range((1 - side) * reach, (2 - side) * reach):
                e = other - row + reach
                inside = 0 <= e < lay.taps
                blocks.append(strip_band(lay, line[e : e + 1], keep_west, keep_east) if inside else nothing)
            rows_of_bands.append(jnp.concatenate(blocks, axis=1))
        source = window[0, (1 - side) * reach : (2 - side) * reach]
        result = product(
            jnp.concatenate(rows_of_bands, axis=0),
            source.reshape(reach * LANES, lay.channels),
            ((1,), (0,)),
        )
        basis_out[side * lay.side : (side + 1) * lay.side] = result.astype(jnp.bfloat16)
    cot = window[1, :, : lay.strip].reshape(2 * lay.side, lay.channels)
    return product(basis_out[...], cot, ((0,), (0,))) * scale


def outer_kernel(lay, scale, near, outer, inner, grad, window, taps, basis_out):
    reach = lay.reach
    even = lax.axis_index("lat") % 2 == 0
    at_outer, at_near = jnp.where(even, 0, reach), jnp.where(even, reach, 0)
    for at, message in ((at_near, near), (at_outer, outer)):
        for row in range(reach):
            for field in range(2):
                start = field * lay.side + row * lay.strip
                put_row(lay, window, field, at + row, message[start : start + lay.strip])
        put_taps(taps, at, reach, message, 2 * lay.side)
    total = inner[...].astype(jnp.float32) + across(lay, scale, window, taps, basis_out)
    grad[...] = total.astype(jnp.bfloat16)


def middle_kernel(lay, scale, near, far, passed, grad, window, taps, basis_out):
    reach = lay.reach
    lat = lax.axis_index("lat")
    upper = (lat // 2) % 2 == 0
    first = lat % 2 == 0
    at_near, at_far = jnp.where(upper, 0, reach), jnp.where(upper, reach, 0)
    for row in range(reach):
        cells = slice(row * lay.strip, (row + 1) * lay.strip)
        put_row(lay, window, 0, at_far + row, jnp.where(first, far[cells], passed[cells]))
        put_row(lay, window, 1, at_far + row, jnp.where(first, passed[cells], far[cells]))
        for field in range(2):
            start = field * lay.side + row * lay.strip
            put_row(lay, window, field, at_near + row, near[start : start + lay.strip])
    put_taps(taps, at_near, reach, near, 2 * lay.side)
    put_taps(taps, at_far, reach, far, lay.side)
    grad[...] = across(lay, scale, window, taps, basis_out)


def field_kernel(
    lay, strip, filters, partner, outer, turned, turned_partner, turned_outer, weight,
    output, field_grad, window, taps, mixed,
):
    rows, reach, width, basis = lay.rows, lay.reach, lay.width, lay.basis
    even = lax.axis_index("lat") % 2 == 0
    at_outer, at_partner = jnp.where(even, 0, rows + reach), jnp.where(even, rows + reach, 0)
    for field in range(2):
        for row in range(rows):
            put_row(lay, window, field, reach + row, strip[field, row])
        for row in range(reach):
            start = (field * rows + row) * lay.strip
            last = start + (rows - reach) * lay.strip
            near = jnp.where(even, partner[start : start + lay.strip], partner[last : last + lay.strip])
            put_row(lay, window, field, at_partner + row, near)
            start = field * lay.side + row * lay.strip
            put_row(lay, window, field, at_outer + row, outer[start : start + lay.strip])

    def bands(row, is_turned):
        blocks = []
        for n in range(lay.taps):
            at, e = (row + n, lay.taps - 1 - n) if is_turned else (reach + row, n)
            parts = []
            for k in range(basis):
                spread = jnp.broadcast_to(taps[at, k, e : e + 1], (width, LANES))
                parts.append(pltpu.roll(spread, int(is_turned), 1, stride=1, stride_axis=0))
            blocks.append(jnp.concatenate(parts, axis=0).astype(jnp.bfloat16))
        return jnp.concatenate(blocks, axis=1)

    def put(at, message, start, count, is_turned):
        both = message[start : start + count * TAP_ROWS].astype(jnp.float32)
        for row in range(count):
            for k in range(basis):
                block = basis - 1 - k if is_turned else k
                taps[at + row, k] = lines(lay, both[row * TAP_ROWS : (row + 1) * TAP_ROWS], block)

    for field, is_turned, out in ((0, False, output), (1, True, field_grad)):
        if is_turned:
            put(reach, turned, 0, rows, True)
            put(at_partner, turned_partner, 0, reach, True)
            put(at_outer, turned_outer, 0, reach, True)
        else:
            put(reach, filters, 0, rows, False)
        for row in range(rows):
            source = window[field, row : row + lay.taps].reshape(lay.taps * LANES, lay.channels)
            result = product(bands(row, is_turned), source, ((1,), (0,))).astype(jnp.bfloat16)
            for k in range(basis):
                mixed[k, row * width : (row + 1) * width] = result[k * width : (k + 1) * width]
        total = jnp.zeros((rows * width, lay.channels), jnp.float32)
        for k in range(basis):
            total += product(mixed[k], weight[k], ((1,), (1 if is_turned else 0,)))
        out[...] = total.astype(jnp.bfloat16).reshape(out.shape)


def widen(part, out, at, wide, sems):
    count = sems.shape[0]
    size = part.shape[0] // count
    copies = []
    for piece in range(count):
        rows = slice(piece * size, (piece + 1) * size)
        wide[rows] = part[rows].astype(jnp.float32)
        target = out.at[pl.ds(pl.multiple_of(at + piece * size, size), size)]
        copies.append(pltpu.make_async_copy(wide.at[rows], target, sems.at[piece]))
        copies[-1].start()
    for copy in copies:
        copy.wait()


def first_kernel(part, out, wide, sems):
    widen(part, out, (lax.axis_index("lat") % 2) * part.shape[0], wide, sems)


def second_kernel(part, kept, out, wide, sems):
    widen(part, out, (1 - lax.axis_index("lat") % 2) * part.shape[0], wide, sems)


def store(part, kept=None):
    rows, channels = part.shape
    vmem, anywhere = pl.BlockSpec(memory_space=pltpu.VMEM), pl.BlockSpec(memory_space=pl.ANY)
    pieces = 4
    return pl.pallas_call(
        first_kernel if kept is None else second_kernel,
        out_shape=jax.ShapeDtypeStruct((2 * rows, channels), jnp.float32),
        in_specs=[vmem] if kept is None else [vmem, anywhere],
        out_specs=anywhere,
        input_output_aliases={} if kept is None else {1: 0},
        scratch_shapes=[pltpu.VMEM((rows, channels), jnp.float32), pltpu.SemaphoreType.DMA((pieces,))],
        compiler_params=pltpu.CompilerParams(vmem_limit_bytes=32 * 1024 * 1024),
        cost_estimate=pl.CostEstimate(flops=1_000_000, bytes_accessed=1_000_000, transcendentals=0),
        name="store_first" if kept is None else "store_second",
    )(*([part] if kept is None else [part, kept]))


def call(kernel, outs, scratch, flops, name):
    vmem = pl.BlockSpec(memory_space=pltpu.VMEM)

    def run(*operands):
        return pl.pallas_call(
            kernel,
            out_shape=outs,
            in_specs=[vmem] * len(operands),
            out_specs=[vmem] * len(outs),
            scratch_shapes=scratch,
            compiler_params=pltpu.CompilerParams(vmem_limit_bytes=32 * 1024 * 1024),
            cost_estimate=pl.CostEstimate(flops=flops, bytes_accessed=1_000_000, transcendentals=0),
            name=name,
        )(*operands)

    return run


def per_device(features, cotangent, weight, filter_taps, lat_ext, lon_count):
    rows, width, channels = features.shape
    basis = weight.shape[0]
    lat_taps = filter_taps.shape[2]
    lay = Layout(rows, lat_taps // 2, width, basis, channels)
    reach = lay.reach
    lat, lon = lax.axis_index("lat"), lax.axis_index("lon")
    even = lat % 2 == 0

    own = jnp.concatenate([features, cotangent], axis=0)
    west = shift(own, "lon", 1)
    own, lat_ext = lax.optimization_barrier((own, lat_ext))
    east = shift(own, "lon", -1)
    filters = make_filters(filter_taps, lat_ext, lon_count)
    filters = jnp.pad(jnp.swapaxes(filters, 1, 2), ((0, 0), (0, TAP_ROWS - lat_taps), (0, 0), (0, 0)))
    filters = filters.reshape(rows * TAP_ROWS, channels)

    strip = jnp.concatenate([west, own, east], axis=1).reshape(2, rows, lay.strip, channels)
    partner = flip(jnp.concatenate([strip.reshape(-1, channels), filters], axis=0), "lat", 1)
    partner_taps = partner[lay.cells :]

    def edge(cells, taps, bottom):
        start = jnp.where(bottom, rows - reach, 0)
        cells = lax.dynamic_slice_in_dim(cells.reshape(strip.shape), start, reach, 1)
        taps = lax.dynamic_slice_in_dim(taps, start * TAP_ROWS, reach * TAP_ROWS, 0)
        return jnp.concatenate([cells.reshape(-1, channels), taps], axis=0)

    upper = (lat // 2) % 2 == 0
    beside = (lat % 2 == 1) == upper
    near = jnp.where(beside, edge(strip, filters, upper), edge(partner[: lay.cells], partner_taps, upper))
    piece = lax.dynamic_slice_in_dim(near, (lat % 2) * lay.side, lay.side, 0)
    far = flip(jnp.concatenate([piece, near[2 * lay.side :]], axis=0), "lat", 2)

    def scratch(window_rows, basis_rows):
        return [
            pltpu.VMEM((2, window_rows, LANES, channels), jnp.bfloat16),
            pltpu.VMEM((window_rows, TAP_ROWS, channels), jnp.float32),
            pltpu.VMEM((basis_rows, channels), jnp.bfloat16),
        ]

    scale = 1.0 / math.sqrt(rows * lax.axis_size("lat") * width * lax.axis_size("lon"))
    share = jax.ShapeDtypeStruct((channels, channels), jnp.bfloat16)
    edges = scratch(2 * reach, 2 * lay.side)
    (grad,) = call(
        functools.partial(inner_kernel, lay, scale),
        [share],
        scratch(2 * rows, 2 * rows * lay.strip),
        INNER_FLOPS,
        "weight_inner",
    )(strip, filters, partner)
    outer = None
    if lax.axis_size("lat") > 4:
        bottom = jnp.logical_not(even)
        outward = edge(strip, filters, bottom)
        outer = outer_swap(outward, "lat")
        (grad,) = call(functools.partial(outer_kernel, lay, scale), [share], edges, MIDDLE_FLOPS, "weight_outer")(
            outward, outer, grad
        )
    got = flip(grad, "lat", 2)
    far, grad = lax.optimization_barrier((far, grad))
    passed = flip(far[: lay.side], "lat", 1)
    (middle,) = call(
        functools.partial(middle_kernel, lay, scale),
        [jax.ShapeDtypeStruct((channels, channels), jnp.float32)],
        edges,
        MIDDLE_FLOPS,
        "weight_middle",
    )(near, far, passed)
    grad = (grad.astype(jnp.float32) + got.astype(jnp.float32) + middle).astype(jnp.bfloat16)

    beyond = jnp.concatenate(
        [jnp.where(even, far[: lay.side], passed), jnp.where(even, passed, far[: lay.side]), far[lay.side :]], axis=0
    )
    outer = jnp.where(beside, beyond, jnp.zeros_like(beyond) if outer is None else outer)
    output, field_grad = call(
        functools.partial(field_kernel, lay),
        [jax.ShapeDtypeStruct(features.shape, jnp.bfloat16)] * 2,
        [
            pltpu.VMEM((2, rows + 2 * reach, LANES, channels), jnp.bfloat16),
            pltpu.VMEM((rows + 2 * reach, basis, TAP_ROWS, LANES), jnp.float32),
            pltpu.VMEM((basis, rows * width, channels), jnp.bfloat16),
        ],
        FIELD_FLOPS,
        "fields",
    )(
        strip,
        filters,
        partner,
        outer,
        filters[:, ::-1],
        edge(partner[: lay.cells], partner_taps, jnp.logical_not(even))[2 * lay.side :, ::-1],
        outer[2 * lay.side :, ::-1],
        weight,
    )

    lat_count, lon_count_devices = lax.axis_size("lat"), lax.axis_size("lon")
    lat_bits = [1 << b for b in range(2, lat_count.bit_length() - 1)]
    lon_bits = [1 << b for b in range(1, lon_count_devices.bit_length() - 1)]
    rounds = [(bit, bit, 0, 0) for bit in lat_bits]
    rounds += [(0, 0, up, down) for up, down in zip(lon_bits, lon_bits[::-1], strict=True)]
    for step, (lat_even, lat_odd, lon_even, lon_odd) in enumerate(rounds):
        if step == 1:
            grad, output, field_grad = lax.optimization_barrier((grad, output, field_grad))
        pairs = []
        for a in range(lat_count):
            lat_bit, lon_bit = (lat_odd, lon_odd) if a % 2 else (lat_even, lon_even)
            for o in range(lon_count_devices):
                pairs.append((a * lon_count_devices + o, (a ^ lat_bit) * lon_count_devices + (o ^ lon_bit)))
        got = lax.ppermute(grad, ("lat", "lon"), pairs)
        grad = (grad.astype(jnp.float32) + got.astype(jnp.float32)).astype(jnp.bfloat16)
    got = flip(grad, "lon", 1)
    second = lon % 2 == 1
    grad = jnp.concatenate([jnp.where(second, got, grad), jnp.where(second, grad, got)], axis=0)
    got = flip(grad, "lat", 1)
    weight_grad = store(got, store(grad)).reshape(basis, channels, channels)
    return (output, field_grad, weight_grad)


def solution(mesh):
    in_specs = (
        P("lat", "lon", None),
        P("lat", "lon", None),
        P(),
        P("lat", None, None, None),
        P("lat"),
        P("lat"),
    )
    out_specs = (P("lat", "lon", None), P("lat", "lon", None), P())
    return jax.shard_map(
        per_device, mesh=mesh, in_specs=in_specs, out_specs=out_specs, check_vma=False
    )
```

```python
import functools
import math

import jax
import jax.numpy as jnp
from jax import lax
from jax.experimental import pallas as pl
from jax.experimental.pallas import tpu as pltpu
from jax.sharding import PartitionSpec as P

LANES = 128
TAP_ROWS = 8
INNER_FLOPS = 300_000_000
MIDDLE_FLOPS = 100_000_000
FIELD_FLOPS = 400_000_000


def shift(block, axis, by):
    count = lax.axis_size(axis)
    return lax.ppermute(block, axis, [(i, (i + by) % count) for i in range(count)])


def flip(block, axis, bit):
    count = lax.axis_size(axis)
    return lax.ppermute(block, axis, [(i, i ^ bit) for i in range(count)])


def outer_swap(block, axis):
    pairs = [(i, i + 1) for i in range(3, lax.axis_size(axis) - 1, 4)]
    return lax.ppermute(block, axis, pairs + [(b, a) for a, b in pairs])


def make_filters(filter_taps, lat_ext, lon_count):
    lat_reach = filter_taps.shape[2] // 2
    half_width = filter_taps.shape[3] // 2
    lat_dist = jnp.abs(jnp.arange(filter_taps.shape[2], dtype=jnp.int32) - lat_reach)
    lon_dist = jnp.abs(jnp.arange(filter_taps.shape[3], dtype=jnp.int32) - half_width)
    support = (lat_dist[None, :, None] < lat_ext[:, None, None]) & (
        lon_dist[None, None, :] < lon_count[:, None, None]
    )
    support_size = ((2 * lat_ext - 1) * (2 * lon_count - 1)).astype(jnp.float32)
    row_scale = lax.rsqrt(support_size)
    masked = (
        filter_taps.astype(jnp.float32)
        * support[:, None].astype(jnp.float32)
        * row_scale[:, None, None, None]
    )
    return masked.astype(jnp.bfloat16)


class Layout:
    def __init__(self, rows, reach, width, basis, channels):
        self.rows, self.reach, self.width = rows, reach, width
        self.basis, self.channels = basis, channels
        self.taps = 2 * reach + 1
        self.strip = 3 * width
        self.cells = 2 * rows * self.strip
        self.side = reach * self.strip


def put_row(lay, window, field, at, cells):
    window[field, at, : lay.strip] = cells
    window[field, at, lay.strip :] = jnp.zeros((LANES - lay.strip, lay.channels), jnp.bfloat16)


def put_taps(taps, at, count, message, start):
    for row in range(0, count, 2):
        both = message[start + row * TAP_ROWS : start + (row + 2) * TAP_ROWS].astype(jnp.float32)
        taps[at + row] = both[:TAP_ROWS]
        taps[at + row + 1] = both[TAP_ROWS:]


def lines(lay, rows_taps, block):
    width = 2 * lay.width
    lanes = rows_taps.shape[1]
    moved = pltpu.roll(rows_taps, lax.rem(lanes - block * width, lanes), 1)[:, :LANES]
    lane = lax.broadcasted_iota(jnp.int32, (1, LANES), 1)
    return jnp.where(lane < width, moved, 0.0)


def my_basis():
    return (lax.axis_index("lat") % 2) * 2 + lax.axis_index("lon") % 2


def strip_band(lay, line, keep_west, keep_east):
    width = lay.width
    middle = pltpu.roll(jnp.broadcast_to(line, (width, LANES)), 0, 1, stride=1, stride_axis=0)
    west = pltpu.roll(middle, LANES - width, 1) * keep_west
    east = pltpu.roll(middle, width, 1) * keep_east
    return jnp.concatenate([west, middle, east], axis=0).astype(jnp.bfloat16)


def keep_lanes(lay):
    even = lax.axis_index("lon") % 2 == 0
    lane = lax.broadcasted_iota(jnp.int32, (1, LANES), 1)
    west = jnp.where((lane < lay.width) & even, 0.0, 1.0)
    east = jnp.where((lane >= 2 * lay.width) & jnp.logical_not(even), 0.0, 1.0)
    return west, east


def product(left, right, dims):
    return lax.dot_general(left, right, (dims, ((), ())), preferred_element_type=jnp.float32)


def inner_kernel(lay, scale, strip, filters, partner, grad, window, taps, basis_out):
    rows, reach = lay.rows, lay.reach
    even = lax.axis_index("lat") % 2 == 0
    at_own, at_partner = jnp.where(even, 0, rows), jnp.where(even, rows, 0)
    for row in range(rows):
        for field in range(2):
            start = (field * rows + row) * lay.strip
            put_row(lay, window, field, at_own + row, strip[field, row])
            put_row(lay, window, field, at_partner + row, partner[start : start + lay.strip])
    put_taps(taps, at_own, rows, filters, 0)
    put_taps(taps, at_partner, rows, partner, lay.cells)
    keep_west, keep_east = keep_lanes(lay)
    mine = my_basis()
    for row in range(2 * rows):
        line = lines(lay, taps[row], mine)
        low, high = max(0, row - reach), min(2 * rows, row + reach + 1)
        bands = [
            strip_band(lay, line[e : e + 1], keep_west, keep_east)
            for e in range(low - row + reach, high - row + reach)
        ]
        source = window[0, low:high].reshape((high - low) * LANES, lay.channels)
        result = product(jnp.concatenate(bands, axis=1), source, ((1,), (0,)))
        basis_out[row * lay.strip : (row + 1) * lay.strip] = result.astype(jnp.bfloat16)
    cot = window[1, :, : lay.strip].reshape(2 * rows * lay.strip, lay.channels)
    grad[...] = (product(basis_out[...], cot, ((0,), (0,))) * scale).astype(jnp.bfloat16)


def across(lay, scale, window, taps, basis_out):
    reach = lay.reach
    keep_west, keep_east = keep_lanes(lay)
    mine = my_basis()
    nothing = jnp.zeros((lay.strip, LANES), jnp.bfloat16)
    for side in range(2):
        rows_of_bands = []
        for row in range(side * reach, (side + 1) * reach):
            line = lines(lay, taps[row], mine)
            blocks = []
            for other in range((1 - side) * reach, (2 - side) * reach):
                e = other - row + reach
                inside = 0 <= e < lay.taps
                blocks.append(strip_band(lay, line[e : e + 1], keep_west, keep_east) if inside else nothing)
            rows_of_bands.append(jnp.concatenate(blocks, axis=1))
        source = window[0, (1 - side) * reach : (2 - side) * reach]
        result = product(
            jnp.concatenate(rows_of_bands, axis=0),
            source.reshape(reach * LANES, lay.channels),
            ((1,), (0,)),
        )
        basis_out[side * lay.side : (side + 1) * lay.side] = result.astype(jnp.bfloat16)
    cot = window[1, :, : lay.strip].reshape(2 * lay.side, lay.channels)
    return product(basis_out[...], cot, ((0,), (0,))) * scale


def outer_kernel(lay, scale, near, outer, inner, grad, window, taps, basis_out):
    reach = lay.reach
    even = lax.axis_index("lat") % 2 == 0
    at_outer, at_near = jnp.where(even, 0, reach), jnp.where(even, reach, 0)
    for at, message in ((at_near, near), (at_outer, outer)):
        for row in range(reach):
            for field in range(2):
                start = field * lay.side + row * lay.strip
                put_row(lay, window, field, at + row, message[start : start + lay.strip])
        put_taps(taps, at, reach, message, 2 * lay.side)
    total = inner[...].astype(jnp.float32) + across(lay, scale, window, taps, basis_out)
    grad[...] = total.astype(jnp.bfloat16)


def middle_kernel(lay, scale, near, far, passed, grad, window, taps, basis_out):
    reach = lay.reach
    lat = lax.axis_index("lat")
    upper = (lat // 2) % 2 == 0
    first = lat % 2 == 0
    at_near, at_far = jnp.where(upper, 0, reach), jnp.where(upper, reach, 0)
    for row in range(reach):
        cells = slice(row * lay.strip, (row + 1) * lay.strip)
        put_row(lay, window, 0, at_far + row, jnp.where(first, far[cells], passed[cells]))
        put_row(lay, window, 1, at_far + row, jnp.where(first, passed[cells], far[cells]))
        for field in range(2):
            start = field * lay.side + row * lay.strip
            put_row(lay, window, field, at_near + row, near[start : start + lay.strip])
    put_taps(taps, at_near, reach, near, 2 * lay.side)
    put_taps(taps, at_far, reach, far, lay.side)
    grad[...] = across(lay, scale, window, taps, basis_out)


def field_kernel(
    lay, strip, filters, partner, outer, turned, turned_partner, turned_outer, weight,
    output, field_grad, window, taps, mixed,
):
    rows, reach, width, basis = lay.rows, lay.reach, lay.width, lay.basis
    even = lax.axis_index("lat") % 2 == 0
    at_outer, at_partner = jnp.where(even, 0, rows + reach), jnp.where(even, rows + reach, 0)
    for field in range(2):
        for row in range(rows):
            put_row(lay, window, field, reach + row, strip[field, row])
        for row in range(reach):
            start = (field * rows + row) * lay.strip
            last = start + (rows - reach) * lay.strip
            near = jnp.where(even, partner[start : start + lay.strip], partner[last : last + lay.strip])
            put_row(lay, window, field, at_partner + row, near)
            start = field * lay.side + row * lay.strip
            put_row(lay, window, field, at_outer + row, outer[start : start + lay.strip])

    def bands(row, is_turned):
        blocks = []
        for n in range(lay.taps):
            at, e = (row + n, lay.taps - 1 - n) if is_turned else (reach + row, n)
            parts = []
            for k in range(basis):
                spread = jnp.broadcast_to(taps[at, k, e : e + 1], (width, LANES))
                parts.append(pltpu.roll(spread, int(is_turned), 1, stride=1, stride_axis=0))
            blocks.append(jnp.concatenate(parts, axis=0).astype(jnp.bfloat16))
        return jnp.concatenate(blocks, axis=1)

    def put(at, message, start, count, is_turned):
        both = message[start : start + count * TAP_ROWS].astype(jnp.float32)
        for row in range(count):
            for k in range(basis):
                block = basis - 1 - k if is_turned else k
                taps[at + row, k] = lines(lay, both[row * TAP_ROWS : (row + 1) * TAP_ROWS], block)

    for field, is_turned, out in ((0, False, output), (1, True, field_grad)):
        if is_turned:
            put(reach, turned, 0, rows, True)
            put(at_partner, turned_partner, 0, reach, True)
            put(at_outer, turned_outer, 0, reach, True)
        else:
            put(reach, filters, 0, rows, False)
        for row in range(rows):
            source = window[field, row : row + lay.taps].reshape(lay.taps * LANES, lay.channels)
            result = product(bands(row, is_turned), source, ((1,), (0,))).astype(jnp.bfloat16)
            for k in range(basis):
                mixed[k, row * width : (row + 1) * width] = result[k * width : (k + 1) * width]
        total = jnp.zeros((rows * width, lay.channels), jnp.float32)
        for k in range(basis):
            total += product(mixed[k], weight[k], ((1,), (1 if is_turned else 0,)))
        out[...] = total.astype(jnp.bfloat16).reshape(out.shape)


def widen(part, out, at, wide, sems):
    count = sems.shape[0]
    size = part.shape[0] // count
    copies = []
    for piece in range(count):
        rows = slice(piece * size, (piece + 1) * size)
        wide[rows] = part[rows].astype(jnp.float32)
        target = out.at[pl.ds(pl.multiple_of(at + piece * size, size), size)]
        copies.append(pltpu.make_async_copy(wide.at[rows], target, sems.at[piece]))
        copies[-1].start()
    for copy in copies:
        copy.wait()


def first_kernel(part, out, wide, sems):
    widen(part, out, (lax.axis_index("lat") % 2) * part.shape[0], wide, sems)


def second_kernel(part, kept, out, wide, sems):
    widen(part, out, (1 - lax.axis_index("lat") % 2) * part.shape[0], wide, sems)


def store(part, kept=None):
    rows, channels = part.shape
    vmem, anywhere = pl.BlockSpec(memory_space=pltpu.VMEM), pl.BlockSpec(memory_space=pl.ANY)
    pieces = 4
    return pl.pallas_call(
        first_kernel if kept is None else second_kernel,
        out_shape=jax.ShapeDtypeStruct((2 * rows, channels), jnp.float32),
        in_specs=[vmem] if kept is None else [vmem, anywhere],
        out_specs=anywhere,
        input_output_aliases={} if kept is None else {1: 0},
        scratch_shapes=[pltpu.VMEM((rows, channels), jnp.float32), pltpu.SemaphoreType.DMA((pieces,))],
        compiler_params=pltpu.CompilerParams(vmem_limit_bytes=32 * 1024 * 1024),
        cost_estimate=pl.CostEstimate(flops=1_000_000, bytes_accessed=1_000_000, transcendentals=0),
        name="store_first" if kept is None else "store_second",
    )(*([part] if kept is None else [part, kept]))


def call(kernel, outs, scratch, flops, name):
    vmem = pl.BlockSpec(memory_space=pltpu.VMEM)

    def run(*operands):
        return pl.pallas_call(
            kernel,
            out_shape=outs,
            in_specs=[vmem] * len(operands),
            out_specs=[vmem] * len(outs),
            scratch_shapes=scratch,
            compiler_params=pltpu.CompilerParams(vmem_limit_bytes=32 * 1024 * 1024),
            cost_estimate=pl.CostEstimate(flops=flops, bytes_accessed=1_000_000, transcendentals=0),
            name=name,
        )(*operands)

    return run


def per_device(features, cotangent, weight, filter_taps, lat_ext, lon_count):
    rows, width, channels = features.shape
    basis = weight.shape[0]
    lat_taps = filter_taps.shape[2]
    lay = Layout(rows, lat_taps // 2, width, basis, channels)
    reach = lay.reach
    lat, lon = lax.axis_index("lat"), lax.axis_index("lon")
    even = lat % 2 == 0

    own = jnp.concatenate([features, cotangent], axis=0)
    west = shift(own, "lon", 1)
    own, lat_ext = lax.optimization_barrier((own, lat_ext))
    east = shift(own, "lon", -1)
    filters = make_filters(filter_taps, lat_ext, lon_count)
    filters = jnp.pad(jnp.swapaxes(filters, 1, 2), ((0, 0), (0, TAP_ROWS - lat_taps), (0, 0), (0, 0)))
    filters = filters.reshape(rows * TAP_ROWS, channels)

    strip = jnp.concatenate([west, own, east], axis=1).reshape(2, rows, lay.strip, channels)
    partner = flip(jnp.concatenate([strip.reshape(-1, channels), filters], axis=0), "lat", 1)
    partner_taps = partner[lay.cells :]

    def edge(cells, taps, bottom):
        start = jnp.where(bottom, rows - reach, 0)
        cells = lax.dynamic_slice_in_dim(cells.reshape(strip.shape), start, reach, 1)
        taps = lax.dynamic_slice_in_dim(taps, start * TAP_ROWS, reach * TAP_ROWS, 0)
        return jnp.concatenate([cells.reshape(-1, channels), taps], axis=0)

    upper = (lat // 2) % 2 == 0
    beside = (lat % 2 == 1) == upper
    near = jnp.where(beside, edge(strip, filters, upper), edge(partner[: lay.cells], partner_taps, upper))
    at = (lat % 2) * rows * lay.strip + jnp.where(upper, rows - reach, 0) * lay.strip
    at_taps = jnp.where(upper, rows - reach, 0) * TAP_ROWS
    piece = jnp.where(
        beside,
        lax.dynamic_slice_in_dim(strip.reshape(-1, channels), at, lay.side, 0),
        lax.dynamic_slice_in_dim(partner, at, lay.side, 0),
    )
    piece_taps = jnp.where(
        beside,
        lax.dynamic_slice_in_dim(filters, at_taps, reach * TAP_ROWS, 0),
        lax.dynamic_slice_in_dim(partner, lay.cells + at_taps, reach * TAP_ROWS, 0),
    )
    far = flip(jnp.concatenate([piece, piece_taps], axis=0), "lat", 2)

    def scratch(window_rows, basis_rows):
        return [
            pltpu.VMEM((2, window_rows, LANES, channels), jnp.bfloat16),
            pltpu.VMEM((window_rows, TAP_ROWS, channels), jnp.float32),
            pltpu.VMEM((basis_rows, channels), jnp.bfloat16),
        ]

    scale = 1.0 / math.sqrt(rows * lax.axis_size("lat") * width * lax.axis_size("lon"))
    share = jax.ShapeDtypeStruct((channels, channels), jnp.bfloat16)
    edges = scratch(2 * reach, 2 * lay.side)
    (grad,) = call(
        functools.partial(inner_kernel, lay, scale),
        [share],
        scratch(2 * rows, 2 * rows * lay.strip),
        INNER_FLOPS,
        "weight_inner",
    )(strip, filters, partner)
    outer = None
    if lax.axis_size("lat") > 4:
        bottom = jnp.logical_not(even)
        outward = edge(strip, filters, bottom)
        outer = outer_swap(outward, "lat")
        (grad,) = call(functools.partial(outer_kernel, lay, scale), [share], edges, MIDDLE_FLOPS, "weight_outer")(
            outward, outer, grad
        )
    got = flip(grad, "lat", 2)
    far, grad = lax.optimization_barrier((far, grad))
    passed = flip(far[: lay.side], "lat", 1)
    (middle,) = call(
        functools.partial(middle_kernel, lay, scale),
        [jax.ShapeDtypeStruct((channels, channels), jnp.float32)],
        edges,
        MIDDLE_FLOPS,
        "weight_middle",
    )(near, far, passed)
    grad = (grad.astype(jnp.float32) + got.astype(jnp.float32) + middle).astype(jnp.bfloat16)

    beyond = jnp.concatenate(
        [jnp.where(even, far[: lay.side], passed), jnp.where(even, passed, far[: lay.side]), far[lay.side :]], axis=0
    )
    outer = jnp.where(beside, beyond, jnp.zeros_like(beyond) if outer is None else outer)
    output, field_grad = call(
        functools.partial(field_kernel, lay),
        [jax.ShapeDtypeStruct(features.shape, jnp.bfloat16)] * 2,
        [
            pltpu.VMEM((2, rows + 2 * reach, LANES, channels), jnp.bfloat16),
            pltpu.VMEM((rows + 2 * reach, basis, TAP_ROWS, LANES), jnp.float32),
            pltpu.VMEM((basis, rows * width, channels), jnp.bfloat16),
        ],
        FIELD_FLOPS,
        "fields",
    )(
        strip,
        filters,
        partner,
        outer,
        filters[:, ::-1],
        edge(partner[: lay.cells], partner_taps, jnp.logical_not(even))[2 * lay.side :, ::-1],
        outer[2 * lay.side :, ::-1],
        weight,
    )

    lat_size, lon_size = lax.axis_size("lat"), lax.axis_size("lon")
    lat_bits = [1 << b for b in range(2, lat_size.bit_length() - 1)]
    lon_bits = [1 << b for b in range(1, lon_size.bit_length() - 1)]
    rounds = [(bit, bit, 0, 0) for bit in lat_bits]
    rounds += [(0, 0, up, down) for up, down in zip(lon_bits, lon_bits[::-1], strict=True)]
    for step, (lat_even, lat_odd, lon_even, lon_odd) in enumerate(rounds):
        if step == 1:
            grad, output, field_grad = lax.optimization_barrier((grad, output, field_grad))
        pairs = []
        for a in range(lat_size):
            lat_bit, lon_bit = (lat_odd, lon_odd) if a % 2 else (lat_even, lon_even)
            for o in range(lon_size):
                pairs.append((a * lon_size + o, (a ^ lat_bit) * lon_size + (o ^ lon_bit)))
        got = lax.ppermute(grad, ("lat", "lon"), pairs)
        grad = (grad.astype(jnp.float32) + got.astype(jnp.float32)).astype(jnp.bfloat16)
    got = flip(grad, "lon", 1)
    second = lon % 2 == 1
    grad = jnp.concatenate([jnp.where(second, got, grad), jnp.where(second, grad, got)], axis=0)
    got = flip(grad, "lat", 1)
    weight_grad = store(got, store(grad)).reshape(basis, channels, channels)
    return (output, field_grad, weight_grad)


def solution(mesh):
    in_specs = (
        P("lat", "lon", None),
        P("lat", "lon", None),
        P(),
        P("lat", None, None, None),
        P("lat"),
        P("lat"),
    )
    out_specs = (P("lat", "lon", None), P("lat", "lon", None), P())
    return jax.shard_map(
        per_device, mesh=mesh, in_specs=in_specs, out_specs=out_specs, check_vma=False
    )
```

```python
import functools
import math

import jax
import jax.numpy as jnp
from jax import lax
from jax.experimental import pallas as pl
from jax.experimental.pallas import tpu as pltpu
from jax.sharding import PartitionSpec as P

LANES = 128
TAP_ROWS = 8
INNER_FLOPS = 300_000_000
MIDDLE_FLOPS = 100_000_000
FIELD_FLOPS = 400_000_000


def shift(block, axis, by):
    count = lax.axis_size(axis)
    return lax.ppermute(block, axis, [(i, (i + by) % count) for i in range(count)])


def flip(block, axis, bit):
    count = lax.axis_size(axis)
    return lax.ppermute(block, axis, [(i, i ^ bit) for i in range(count)])


def outer_swap(block, axis):
    pairs = [(i, i + 1) for i in range(3, lax.axis_size(axis) - 1, 4)]
    return lax.ppermute(block, axis, pairs + [(b, a) for a, b in pairs])


def make_filters(filter_taps, lat_ext, lon_count):
    lat_reach = filter_taps.shape[2] // 2
    half_width = filter_taps.shape[3] // 2
    lat_dist = jnp.abs(jnp.arange(filter_taps.shape[2], dtype=jnp.int32) - lat_reach)
    lon_dist = jnp.abs(jnp.arange(filter_taps.shape[3], dtype=jnp.int32) - half_width)
    support = (lat_dist[None, :, None] < lat_ext[:, None, None]) & (
        lon_dist[None, None, :] < lon_count[:, None, None]
    )
    support_size = ((2 * lat_ext - 1) * (2 * lon_count - 1)).astype(jnp.float32)
    row_scale = lax.rsqrt(support_size)
    masked = (
        filter_taps.astype(jnp.float32)
        * support[:, None].astype(jnp.float32)
        * row_scale[:, None, None, None]
    )
    return masked.astype(jnp.bfloat16)


class Layout:
    def __init__(self, rows, reach, width, basis, channels):
        self.rows, self.reach, self.width = rows, reach, width
        self.basis, self.channels = basis, channels
        self.taps = 2 * reach + 1
        self.strip = 3 * width
        self.cells = 2 * rows * self.strip
        self.side = reach * self.strip


def put_row(lay, window, field, at, cells):
    window[field, at, : lay.strip] = cells
    window[field, at, lay.strip :] = jnp.zeros((LANES - lay.strip, lay.channels), jnp.bfloat16)


def put_taps(taps, at, count, message, start):
    for row in range(0, count, 2):
        both = message[start + row * TAP_ROWS : start + (row + 2) * TAP_ROWS].astype(jnp.float32)
        taps[at + row] = both[:TAP_ROWS]
        taps[at + row + 1] = both[TAP_ROWS:]


def lines(lay, rows_taps, block):
    width = 2 * lay.width
    lanes = rows_taps.shape[1]
    moved = pltpu.roll(rows_taps, lax.rem(lanes - block * width, lanes), 1)[:, :LANES]
    lane = lax.broadcasted_iota(jnp.int32, (1, LANES), 1)
    return jnp.where(lane < width, moved, 0.0)


def my_basis():
    return (lax.axis_index("lat") % 2) * 2 + lax.axis_index("lon") % 2


def strip_band(lay, line, keep_west, keep_east):
    width = lay.width
    middle = pltpu.roll(jnp.broadcast_to(line, (width, LANES)), 0, 1, stride=1, stride_axis=0)
    west = pltpu.roll(middle, LANES - width, 1) * keep_west
    east = pltpu.roll(middle, width, 1) * keep_east
    return jnp.concatenate([west, middle, east], axis=0).astype(jnp.bfloat16)


def keep_lanes(lay):
    even = lax.axis_index("lon") % 2 == 0
    lane = lax.broadcasted_iota(jnp.int32, (1, LANES), 1)
    west = jnp.where((lane < lay.width) & even, 0.0, 1.0)
    east = jnp.where((lane >= 2 * lay.width) & jnp.logical_not(even), 0.0, 1.0)
    return west, east


def product(left, right, dims):
    return lax.dot_general(left, right, (dims, ((), ())), preferred_element_type=jnp.float32)


def inner_kernel(lay, scale, strip, filters, partner, grad, window, taps, basis_out):
    rows, reach = lay.rows, lay.reach
    even = lax.axis_index("lat") % 2 == 0
    at_own, at_partner = jnp.where(even, 0, rows), jnp.where(even, rows, 0)
    for row in range(rows):
        for field in range(2):
            start = (field * rows + row) * lay.strip
            put_row(lay, window, field, at_own + row, strip[field, row])
            put_row(lay, window, field, at_partner + row, partner[start : start + lay.strip])
    put_taps(taps, at_own, rows, filters, 0)
    put_taps(taps, at_partner, rows, partner, lay.cells)
    keep_west, keep_east = keep_lanes(lay)
    mine = my_basis()
    for row in range(2 * rows):
        line = lines(lay, taps[row], mine)
        low, high = max(0, row - reach), min(2 * rows, row + reach + 1)
        bands = [
            strip_band(lay, line[e : e + 1], keep_west, keep_east)
            for e in range(low - row + reach, high - row + reach)
        ]
        source = window[0, low:high].reshape((high - low) * LANES, lay.channels)
        result = product(jnp.concatenate(bands, axis=1), source, ((1,), (0,)))
        basis_out[row * lay.strip : (row + 1) * lay.strip] = result.astype(jnp.bfloat16)
    cot = window[1, :, : lay.strip].reshape(2 * rows * lay.strip, lay.channels)
    grad[...] = (product(basis_out[...], cot, ((0,), (0,))) * scale).astype(jnp.bfloat16)


def across(lay, scale, window, taps, basis_out):
    reach = lay.reach
    keep_west, keep_east = keep_lanes(lay)
    mine = my_basis()
    nothing = jnp.zeros((lay.strip, LANES), jnp.bfloat16)
    for side in range(2):
        rows_of_bands = []
        for row in range(side * reach, (side + 1) * reach):
            line = lines(lay, taps[row], mine)
            blocks = []
            for other in range((1 - side) * reach, (2 - side) * reach):
                e = other - row + reach
                inside = 0 <= e < lay.taps
                blocks.append(strip_band(lay, line[e : e + 1], keep_west, keep_east) if inside else nothing)
            rows_of_bands.append(jnp.concatenate(blocks, axis=1))
        source = window[0, (1 - side) * reach : (2 - side) * reach]
        result = product(
            jnp.concatenate(rows_of_bands, axis=0),
            source.reshape(reach * LANES, lay.channels),
            ((1,), (0,)),
        )
        basis_out[side * lay.side : (side + 1) * lay.side] = result.astype(jnp.bfloat16)
    cot = window[1, :, : lay.strip].reshape(2 * lay.side, lay.channels)
    return product(basis_out[...], cot, ((0,), (0,))) * scale


def outer_kernel(lay, scale, near, outer, inner, grad, window, taps, basis_out):
    reach = lay.reach
    even = lax.axis_index("lat") % 2 == 0
    at_outer, at_near = jnp.where(even, 0, reach), jnp.where(even, reach, 0)
    for at, message in ((at_near, near), (at_outer, outer)):
        for row in range(reach):
            for field in range(2):
                start = field * lay.side + row * lay.strip
                put_row(lay, window, field, at + row, message[start : start + lay.strip])
        put_taps(taps, at, reach, message, 2 * lay.side)
    total = inner[...].astype(jnp.float32) + across(lay, scale, window, taps, basis_out)
    grad[...] = total.astype(jnp.bfloat16)


def middle_kernel(lay, scale, near, far, passed, grad, window, taps, basis_out):
    reach = lay.reach
    lat = lax.axis_index("lat")
    upper = (lat // 2) % 2 == 0
    first = lat % 2 == 0
    at_near, at_far = jnp.where(upper, 0, reach), jnp.where(upper, reach, 0)
    for row in range(reach):
        cells = slice(row * lay.strip, (row + 1) * lay.strip)
        put_row(lay, window, 0, at_far + row, jnp.where(first, far[cells], passed[cells]))
        put_row(lay, window, 1, at_far + row, jnp.where(first, passed[cells], far[cells]))
        for field in range(2):
            start = field * lay.side + row * lay.strip
            put_row(lay, window, field, at_near + row, near[start : start + lay.strip])
    put_taps(taps, at_near, reach, near, 2 * lay.side)
    put_taps(taps, at_far, reach, far, lay.side)
    grad[...] = across(lay, scale, window, taps, basis_out)


def field_kernel(
    lay, strip, filters, partner, outer, turned, turned_partner, turned_outer, weight,
    output, field_grad, window, taps, mixed,
):
    rows, reach, width, basis = lay.rows, lay.reach, lay.width, lay.basis
    even = lax.axis_index("lat") % 2 == 0
    at_outer, at_partner = jnp.where(even, 0, rows + reach), jnp.where(even, rows + reach, 0)
    for field in range(2):
        for row in range(rows):
            put_row(lay, window, field, reach + row, strip[field, row])
        for row in range(reach):
            start = (field * rows + row) * lay.strip
            last = start + (rows - reach) * lay.strip
            near = jnp.where(even, partner[start : start + lay.strip], partner[last : last + lay.strip])
            put_row(lay, window, field, at_partner + row, near)
            start = field * lay.side + row * lay.strip
            put_row(lay, window, field, at_outer + row, outer[start : start + lay.strip])

    def bands(row, is_turned):
        blocks = []
        for n in range(lay.taps):
            at, e = (row + n, lay.taps - 1 - n) if is_turned else (reach + row, n)
            parts = []
            for k in range(basis):
                spread = jnp.broadcast_to(taps[at, k, e : e + 1], (width, LANES))
                parts.append(pltpu.roll(spread, int(is_turned), 1, stride=1, stride_axis=0))
            blocks.append(jnp.concatenate(parts, axis=0).astype(jnp.bfloat16))
        return jnp.concatenate(blocks, axis=1)

    def put(at, message, start, count, is_turned):
        both = message[start : start + count * TAP_ROWS].astype(jnp.float32)
        for row in range(count):
            for k in range(basis):
                block = basis - 1 - k if is_turned else k
                taps[at + row, k] = lines(lay, both[row * TAP_ROWS : (row + 1) * TAP_ROWS], block)

    for field, is_turned, out in ((0, False, output), (1, True, field_grad)):
        if is_turned:
            put(reach, turned, 0, rows, True)
            put(at_partner, turned_partner, 0, reach, True)
            put(at_outer, turned_outer, 0, reach, True)
        else:
            put(reach, filters, 0, rows, False)
        for row in range(rows):
            source = window[field, row : row + lay.taps].reshape(lay.taps * LANES, lay.channels)
            result = product(bands(row, is_turned), source, ((1,), (0,))).astype(jnp.bfloat16)
            for k in range(basis):
                mixed[k, row * width : (row + 1) * width] = result[k * width : (k + 1) * width]
        total = jnp.zeros((rows * width, lay.channels), jnp.float32)
        for k in range(basis):
            total += product(mixed[k], weight[k], ((1,), (1 if is_turned else 0,)))
        out[...] = total.astype(jnp.bfloat16).reshape(out.shape)


def widen(part, out, at, wide, sems):
    count = sems.shape[0]
    size = part.shape[0] // count
    copies = []
    for piece in range(count):
        rows = slice(piece * size, (piece + 1) * size)
        wide[rows] = part[rows].astype(jnp.float32)
        target = out.at[pl.ds(pl.multiple_of(at + piece * size, size), size)]
        copies.append(pltpu.make_async_copy(wide.at[rows], target, sems.at[piece]))
        copies[-1].start()
    for copy in copies:
        copy.wait()


def first_kernel(part, out, wide, sems):
    widen(part, out, (lax.axis_index("lat") % 2) * part.shape[0], wide, sems)


def second_kernel(part, kept, out, wide, sems):
    widen(part, out, (1 - lax.axis_index("lat") % 2) * part.shape[0], wide, sems)


def store(part, kept=None):
    rows, channels = part.shape
    vmem, anywhere = pl.BlockSpec(memory_space=pltpu.VMEM), pl.BlockSpec(memory_space=pl.ANY)
    pieces = 4
    return pl.pallas_call(
        first_kernel if kept is None else second_kernel,
        out_shape=jax.ShapeDtypeStruct((2 * rows, channels), jnp.float32),
        in_specs=[vmem] if kept is None else [vmem, anywhere],
        out_specs=anywhere,
        input_output_aliases={} if kept is None else {1: 0},
        scratch_shapes=[pltpu.VMEM((rows, channels), jnp.float32), pltpu.SemaphoreType.DMA((pieces,))],
        compiler_params=pltpu.CompilerParams(vmem_limit_bytes=32 * 1024 * 1024),
        cost_estimate=pl.CostEstimate(flops=1_000_000, bytes_accessed=1_000_000, transcendentals=0),
        name="store_first" if kept is None else "store_second",
    )(*([part] if kept is None else [part, kept]))


def call(kernel, outs, scratch, flops, name):
    vmem = pl.BlockSpec(memory_space=pltpu.VMEM)

    def run(*operands):
        return pl.pallas_call(
            kernel,
            out_shape=outs,
            in_specs=[vmem] * len(operands),
            out_specs=[vmem] * len(outs),
            scratch_shapes=scratch,
            compiler_params=pltpu.CompilerParams(vmem_limit_bytes=32 * 1024 * 1024),
            cost_estimate=pl.CostEstimate(flops=flops, bytes_accessed=1_000_000, transcendentals=0),
            name=name,
        )(*operands)

    return run


def per_device(features, cotangent, weight, filter_taps, lat_ext, lon_count):
    rows, width, channels = features.shape
    basis = weight.shape[0]
    lat_taps = filter_taps.shape[2]
    lay = Layout(rows, lat_taps // 2, width, basis, channels)
    reach = lay.reach
    lat, lon = lax.axis_index("lat"), lax.axis_index("lon")
    even = lat % 2 == 0

    own = jnp.concatenate([features, cotangent], axis=0)
    west = shift(own, "lon", 1)
    own, lat_ext = lax.optimization_barrier((own, lat_ext))
    east = shift(own, "lon", -1)
    filters = make_filters(filter_taps, lat_ext, lon_count)
    filters = jnp.pad(jnp.swapaxes(filters, 1, 2), ((0, 0), (0, TAP_ROWS - lat_taps), (0, 0), (0, 0)))
    filters = filters.reshape(rows * TAP_ROWS, channels)

    late, filters = lax.optimization_barrier((own, filters))
    ahead = flip(late, "lat", 1)
    strip = jnp.concatenate([west, own, east], axis=1).reshape(2, rows, lay.strip, channels)
    message = jnp.concatenate([west.reshape(-1, channels), east.reshape(-1, channels), filters], axis=0)
    message, ahead = lax.optimization_barrier((message, ahead))
    sides = flip(message, "lat", 1)
    part = 2 * rows * width
    partner_taps = sides[2 * part :]
    partner = jnp.concatenate(
        [sides[:part].reshape(own.shape), ahead, sides[part : 2 * part].reshape(own.shape)], axis=1
    ).reshape(-1, channels)
    partner = jnp.concatenate([partner, partner_taps], axis=0)

    def edge(cells, taps, bottom):
        start = jnp.where(bottom, rows - reach, 0)
        cells = lax.dynamic_slice_in_dim(cells.reshape(strip.shape), start, reach, 1)
        taps = lax.dynamic_slice_in_dim(taps, start * TAP_ROWS, reach * TAP_ROWS, 0)
        return jnp.concatenate([cells.reshape(-1, channels), taps], axis=0)

    upper = (lat // 2) % 2 == 0
    beside = (lat % 2 == 1) == upper
    near = jnp.where(beside, edge(strip, filters, upper), edge(partner[: lay.cells], partner_taps, upper))
    at = (lat % 2) * rows * lay.strip + jnp.where(upper, rows - reach, 0) * lay.strip
    at_taps = jnp.where(upper, rows - reach, 0) * TAP_ROWS
    piece = jnp.where(
        beside,
        lax.dynamic_slice_in_dim(strip.reshape(-1, channels), at, lay.side, 0),
        lax.dynamic_slice_in_dim(partner, at, lay.side, 0),
    )
    piece_taps = jnp.where(
        beside,
        lax.dynamic_slice_in_dim(filters, at_taps, reach * TAP_ROWS, 0),
        lax.dynamic_slice_in_dim(partner, lay.cells + at_taps, reach * TAP_ROWS, 0),
    )
    far = flip(jnp.concatenate([piece, piece_taps], axis=0), "lat", 2)

    def scratch(window_rows, basis_rows):
        return [
            pltpu.VMEM((2, window_rows, LANES, channels), jnp.bfloat16),
            pltpu.VMEM((window_rows, TAP_ROWS, channels), jnp.float32),
            pltpu.VMEM((basis_rows, channels), jnp.bfloat16),
        ]

    scale = 1.0 / math.sqrt(rows * lax.axis_size("lat") * width * lax.axis_size("lon"))
    share = jax.ShapeDtypeStruct((channels, channels), jnp.bfloat16)
    edges = scratch(2 * reach, 2 * lay.side)
    (grad,) = call(
        functools.partial(inner_kernel, lay, scale),
        [share],
        scratch(2 * rows, 2 * rows * lay.strip),
        INNER_FLOPS,
        "weight_inner",
    )(strip, filters, partner)
    outer = None
    if lax.axis_size("lat") > 4:
        bottom = jnp.logical_not(even)
        outward = edge(strip, filters, bottom)
        outer = outer_swap(outward, "lat")
        (grad,) = call(functools.partial(outer_kernel, lay, scale), [share], edges, MIDDLE_FLOPS, "weight_outer")(
            outward, outer, grad
        )
    got = flip(grad, "lat", 2)
    far, grad = lax.optimization_barrier((far, grad))
    passed = flip(far[: lay.side], "lat", 1)
    (middle,) = call(
        functools.partial(middle_kernel, lay, scale),
        [jax.ShapeDtypeStruct((channels, channels), jnp.float32)],
        edges,
        MIDDLE_FLOPS,
        "weight_middle",
    )(near, far, passed)
    grad = (grad.astype(jnp.float32) + got.astype(jnp.float32) + middle).astype(jnp.bfloat16)

    beyond = jnp.concatenate(
        [jnp.where(even, far[: lay.side], passed), jnp.where(even, passed, far[: lay.side]), far[lay.side :]], axis=0
    )
    outer = jnp.where(beside, beyond, jnp.zeros_like(beyond) if outer is None else outer)
    output, field_grad = call(
        functools.partial(field_kernel, lay),
        [jax.ShapeDtypeStruct(features.shape, jnp.bfloat16)] * 2,
        [
            pltpu.VMEM((2, rows + 2 * reach, LANES, channels), jnp.bfloat16),
            pltpu.VMEM((rows + 2 * reach, basis, TAP_ROWS, LANES), jnp.float32),
            pltpu.VMEM((basis, rows * width, channels), jnp.bfloat16),
        ],
        FIELD_FLOPS,
        "fields",
    )(
        strip,
        filters,
        partner,
        outer,
        filters[:, ::-1],
        edge(partner[: lay.cells], partner_taps, jnp.logical_not(even))[2 * lay.side :, ::-1],
        outer[2 * lay.side :, ::-1],
        weight,
    )

    lat_size, lon_size = lax.axis_size("lat"), lax.axis_size("lon")
    lat_bits = [1 << b for b in range(2, lat_size.bit_length() - 1)]
    lon_bits = [1 << b for b in range(1, lon_size.bit_length() - 1)]
    rounds = [(bit, bit, 0, 0) for bit in lat_bits]
    rounds += [(0, 0, up, down) for up, down in zip(lon_bits, lon_bits[::-1], strict=True)]
    for step, (lat_even, lat_odd, lon_even, lon_odd) in enumerate(rounds):
        if step == 1:
            grad, output, field_grad = lax.optimization_barrier((grad, output, field_grad))
        pairs = []
        for a in range(lat_size):
            lat_bit, lon_bit = (lat_odd, lon_odd) if a % 2 else (lat_even, lon_even)
            for o in range(lon_size):
                pairs.append((a * lon_size + o, (a ^ lat_bit) * lon_size + (o ^ lon_bit)))
        got = lax.ppermute(grad, ("lat", "lon"), pairs)
        grad = (grad.astype(jnp.float32) + got.astype(jnp.float32)).astype(jnp.bfloat16)
    got = flip(grad, "lon", 1)
    second = lon % 2 == 1
    grad = jnp.concatenate([jnp.where(second, got, grad), jnp.where(second, grad, got)], axis=0)
    got = flip(grad, "lat", 1)
    weight_grad = store(got, store(grad)).reshape(basis, channels, channels)
    return (output, field_grad, weight_grad)


def solution(mesh):
    in_specs = (
        P("lat", "lon", None),
        P("lat", "lon", None),
        P(),
        P("lat", None, None, None),
        P("lat"),
        P("lat"),
    )
    out_specs = (P("lat", "lon", None), P("lat", "lon", None), P())
    return jax.shard_map(
        per_device, mesh=mesh, in_specs=in_specs, out_specs=out_specs, check_vma=False
    )
```

```python
import functools
import math

import jax
import jax.numpy as jnp
from jax import lax
from jax.experimental import pallas as pl
from jax.experimental.pallas import tpu as pltpu
from jax.sharding import PartitionSpec as P

LANES = 128
TAP_ROWS = 8
INNER_FLOPS = 300_000_000
MIDDLE_FLOPS = 100_000_000
FIELD_FLOPS = 400_000_000


def shift(block, axis, by):
    count = lax.axis_size(axis)
    return lax.ppermute(block, axis, [(i, (i + by) % count) for i in range(count)])


def flip(block, axis, bit):
    count = lax.axis_size(axis)
    return lax.ppermute(block, axis, [(i, i ^ bit) for i in range(count)])


def outer_swap(block, axis):
    pairs = [(i, i + 1) for i in range(3, lax.axis_size(axis) - 1, 4)]
    return lax.ppermute(block, axis, pairs + [(b, a) for a, b in pairs])


def make_filters(filter_taps, lat_ext, lon_count):
    lat_reach = filter_taps.shape[2] // 2
    half_width = filter_taps.shape[3] // 2
    lat_dist = jnp.abs(jnp.arange(filter_taps.shape[2], dtype=jnp.int32) - lat_reach)
    lon_dist = jnp.abs(jnp.arange(filter_taps.shape[3], dtype=jnp.int32) - half_width)
    support = (lat_dist[None, :, None] < lat_ext[:, None, None]) & (
        lon_dist[None, None, :] < lon_count[:, None, None]
    )
    support_size = ((2 * lat_ext - 1) * (2 * lon_count - 1)).astype(jnp.float32)
    row_scale = lax.rsqrt(support_size)
    masked = (
        filter_taps.astype(jnp.float32)
        * support[:, None].astype(jnp.float32)
        * row_scale[:, None, None, None]
    )
    return masked.astype(jnp.bfloat16)


class Layout:
    def __init__(self, rows, reach, width, basis, channels):
        self.rows, self.reach, self.width = rows, reach, width
        self.basis, self.channels = basis, channels
        self.taps = 2 * reach + 1
        self.strip = 3 * width
        self.cells = 2 * rows * self.strip
        self.side = reach * self.strip


def put_row(lay, window, field, at, cells):
    window[field, at, : lay.strip] = cells
    window[field, at, lay.strip :] = jnp.zeros((LANES - lay.strip, lay.channels), jnp.bfloat16)


def put_taps(taps, at, count, message, start):
    for row in range(0, count, 2):
        both = message[start + row * TAP_ROWS : start + (row + 2) * TAP_ROWS].astype(jnp.float32)
        taps[at + row] = both[:TAP_ROWS]
        taps[at + row + 1] = both[TAP_ROWS:]


def lines(lay, rows_taps, block):
    width = 2 * lay.width
    lanes = rows_taps.shape[1]
    moved = pltpu.roll(rows_taps, lax.rem(lanes - block * width, lanes), 1)[:, :LANES]
    lane = lax.broadcasted_iota(jnp.int32, (1, LANES), 1)
    return jnp.where(lane < width, moved, 0.0)


def my_basis():
    return (lax.axis_index("lat") % 2) * 2 + lax.axis_index("lon") % 2


def strip_band(lay, line, keep_west, keep_east):
    width = lay.width
    middle = pltpu.roll(jnp.broadcast_to(line, (width, LANES)), 0, 1, stride=1, stride_axis=0)
    west = pltpu.roll(middle, LANES - width, 1) * keep_west
    east = pltpu.roll(middle, width, 1) * keep_east
    return jnp.concatenate([west, middle, east], axis=0).astype(jnp.bfloat16)


def keep_lanes(lay):
    even = lax.axis_index("lon") % 2 == 0
    lane = lax.broadcasted_iota(jnp.int32, (1, LANES), 1)
    west = jnp.where((lane < lay.width) & even, 0.0, 1.0)
    east = jnp.where((lane >= 2 * lay.width) & jnp.logical_not(even), 0.0, 1.0)
    return west, east


def product(left, right, dims):
    return lax.dot_general(left, right, (dims, ((), ())), preferred_element_type=jnp.float32)


def inner_kernel(lay, scale, strip, filters, partner, grad, window, taps, basis_out):
    rows, reach = lay.rows, lay.reach
    even = lax.axis_index("lat") % 2 == 0
    at_own, at_partner = jnp.where(even, 0, rows), jnp.where(even, rows, 0)
    for row in range(rows):
        for field in range(2):
            start = (field * rows + row) * lay.strip
            put_row(lay, window, field, at_own + row, strip[field, row])
            put_row(lay, window, field, at_partner + row, partner[start : start + lay.strip])
    put_taps(taps, at_own, rows, filters, 0)
    put_taps(taps, at_partner, rows, partner, lay.cells)
    keep_west, keep_east = keep_lanes(lay)
    mine = my_basis()
    for row in range(2 * rows):
        line = lines(lay, taps[row], mine)
        low, high = max(0, row - reach), min(2 * rows, row + reach + 1)
        bands = [
            strip_band(lay, line[e : e + 1], keep_west, keep_east)
            for e in range(low - row + reach, high - row + reach)
        ]
        source = window[0, low:high].reshape((high - low) * LANES, lay.channels)
        result = product(jnp.concatenate(bands, axis=1), source, ((1,), (0,)))
        basis_out[row * lay.strip : (row + 1) * lay.strip] = result.astype(jnp.bfloat16)
    cot = window[1, :, : lay.strip].reshape(2 * rows * lay.strip, lay.channels)
    grad[...] = (product(basis_out[...], cot, ((0,), (0,))) * scale).astype(jnp.bfloat16)


def across(lay, scale, window, taps, basis_out):
    reach = lay.reach
    keep_west, keep_east = keep_lanes(lay)
    mine = my_basis()
    nothing = jnp.zeros((lay.strip, LANES), jnp.bfloat16)
    for side in range(2):
        rows_of_bands = []
        for row in range(side * reach, (side + 1) * reach):
            line = lines(lay, taps[row], mine)
            blocks = []
            for other in range((1 - side) * reach, (2 - side) * reach):
                e = other - row + reach
                inside = 0 <= e < lay.taps
                blocks.append(strip_band(lay, line[e : e + 1], keep_west, keep_east) if inside else nothing)
            rows_of_bands.append(jnp.concatenate(blocks, axis=1))
        source = window[0, (1 - side) * reach : (2 - side) * reach]
        result = product(
            jnp.concatenate(rows_of_bands, axis=0),
            source.reshape(reach * LANES, lay.channels),
            ((1,), (0,)),
        )
        basis_out[side * lay.side : (side + 1) * lay.side] = result.astype(jnp.bfloat16)
    cot = window[1, :, : lay.strip].reshape(2 * lay.side, lay.channels)
    return product(basis_out[...], cot, ((0,), (0,))) * scale


def outer_kernel(lay, scale, near, outer, inner, grad, window, taps, basis_out):
    reach = lay.reach
    even = lax.axis_index("lat") % 2 == 0
    at_outer, at_near = jnp.where(even, 0, reach), jnp.where(even, reach, 0)
    for at, message in ((at_near, near), (at_outer, outer)):
        for row in range(reach):
            for field in range(2):
                start = field * lay.side + row * lay.strip
                put_row(lay, window, field, at + row, message[start : start + lay.strip])
        put_taps(taps, at, reach, message, 2 * lay.side)
    total = inner[...].astype(jnp.float32) + across(lay, scale, window, taps, basis_out)
    grad[...] = total.astype(jnp.bfloat16)


def middle_kernel(lay, scale, near, far, passed, grad, window, taps, basis_out):
    reach = lay.reach
    lat = lax.axis_index("lat")
    upper = (lat // 2) % 2 == 0
    first = lat % 2 == 0
    at_near, at_far = jnp.where(upper, 0, reach), jnp.where(upper, reach, 0)
    for row in range(reach):
        cells = slice(row * lay.strip, (row + 1) * lay.strip)
        put_row(lay, window, 0, at_far + row, jnp.where(first, far[cells], passed[cells]))
        put_row(lay, window, 1, at_far + row, jnp.where(first, passed[cells], far[cells]))
        for field in range(2):
            start = field * lay.side + row * lay.strip
            put_row(lay, window, field, at_near + row, near[start : start + lay.strip])
    put_taps(taps, at_near, reach, near, 2 * lay.side)
    put_taps(taps, at_far, reach, far, lay.side)
    grad[...] = across(lay, scale, window, taps, basis_out)


def field_kernel(
    lay, strip, filters, partner, outer, turned, turned_partner, turned_outer, weight,
    output, field_grad, window, taps, mixed,
):
    rows, reach, width, basis = lay.rows, lay.reach, lay.width, lay.basis
    even = lax.axis_index("lat") % 2 == 0
    at_outer, at_partner = jnp.where(even, 0, rows + reach), jnp.where(even, rows + reach, 0)
    for field in range(2):
        for row in range(rows):
            put_row(lay, window, field, reach + row, strip[field, row])
        for row in range(reach):
            start = (field * rows + row) * lay.strip
            last = start + (rows - reach) * lay.strip
            near = jnp.where(even, partner[start : start + lay.strip], partner[last : last + lay.strip])
            put_row(lay, window, field, at_partner + row, near)
            start = field * lay.side + row * lay.strip
            put_row(lay, window, field, at_outer + row, outer[start : start + lay.strip])

    def bands(row, is_turned):
        blocks = []
        for n in range(lay.taps):
            at, e = (row + n, lay.taps - 1 - n) if is_turned else (reach + row, n)
            parts = []
            for k in range(basis):
                spread = jnp.broadcast_to(taps[at, k, e : e + 1], (width, LANES))
                parts.append(pltpu.roll(spread, int(is_turned), 1, stride=1, stride_axis=0))
            blocks.append(jnp.concatenate(parts, axis=0).astype(jnp.bfloat16))
        return jnp.concatenate(blocks, axis=1)

    def put(at, message, start, count, is_turned):
        both = message[start : start + count * TAP_ROWS].astype(jnp.float32)
        for row in range(count):
            for k in range(basis):
                block = basis - 1 - k if is_turned else k
                taps[at + row, k] = lines(lay, both[row * TAP_ROWS : (row + 1) * TAP_ROWS], block)

    for field, is_turned, out in ((0, False, output), (1, True, field_grad)):
        if is_turned:
            put(reach, turned, 0, rows, True)
            put(at_partner, turned_partner, 0, reach, True)
            put(at_outer, turned_outer, 0, reach, True)
        else:
            put(reach, filters, 0, rows, False)
        for row in range(rows):
            source = window[field, row : row + lay.taps].reshape(lay.taps * LANES, lay.channels)
            result = product(bands(row, is_turned), source, ((1,), (0,))).astype(jnp.bfloat16)
            for k in range(basis):
                mixed[k, row * width : (row + 1) * width] = result[k * width : (k + 1) * width]
        total = jnp.zeros((rows * width, lay.channels), jnp.float32)
        for k in range(basis):
            total += product(mixed[k], weight[k], ((1,), (1 if is_turned else 0,)))
        out[...] = total.astype(jnp.bfloat16).reshape(out.shape)


def widen(part, out, at, wide, sems):
    count = sems.shape[0]
    size = part.shape[0] // count
    copies = []
    for piece in range(count):
        rows = slice(piece * size, (piece + 1) * size)
        wide[rows] = part[rows].astype(jnp.float32)
        target = out.at[pl.ds(pl.multiple_of(at + piece * size, size), size)]
        copies.append(pltpu.make_async_copy(wide.at[rows], target, sems.at[piece]))
        copies[-1].start()
    for copy in copies:
        copy.wait()


def first_kernel(part, out, wide, sems):
    widen(part, out, (lax.axis_index("lat") % 2) * part.shape[0], wide, sems)


def second_kernel(part, kept, out, wide, sems):
    widen(part, out, (1 - lax.axis_index("lat") % 2) * part.shape[0], wide, sems)


def store(part, kept=None):
    rows, channels = part.shape
    vmem, anywhere = pl.BlockSpec(memory_space=pltpu.VMEM), pl.BlockSpec(memory_space=pl.ANY)
    pieces = 2
    return pl.pallas_call(
        first_kernel if kept is None else second_kernel,
        out_shape=jax.ShapeDtypeStruct((2 * rows, channels), jnp.float32),
        in_specs=[vmem] if kept is None else [vmem, anywhere],
        out_specs=anywhere,
        input_output_aliases={} if kept is None else {1: 0},
        scratch_shapes=[pltpu.VMEM((rows, channels), jnp.float32), pltpu.SemaphoreType.DMA((pieces,))],
        compiler_params=pltpu.CompilerParams(vmem_limit_bytes=32 * 1024 * 1024),
        cost_estimate=pl.CostEstimate(flops=1_000_000, bytes_accessed=1_000_000, transcendentals=0),
        name="store_first" if kept is None else "store_second",
    )(*([part] if kept is None else [part, kept]))


def call(kernel, outs, scratch, flops, name):
    vmem = pl.BlockSpec(memory_space=pltpu.VMEM)

    def run(*operands):
        return pl.pallas_call(
            kernel,
            out_shape=outs,
            in_specs=[vmem] * len(operands),
            out_specs=[vmem] * len(outs),
            scratch_shapes=scratch,
            compiler_params=pltpu.CompilerParams(vmem_limit_bytes=32 * 1024 * 1024),
            cost_estimate=pl.CostEstimate(flops=flops, bytes_accessed=1_000_000, transcendentals=0),
            name=name,
        )(*operands)

    return run


def per_device(features, cotangent, weight, filter_taps, lat_ext, lon_count):
    rows, width, channels = features.shape
    basis = weight.shape[0]
    lat_taps = filter_taps.shape[2]
    lay = Layout(rows, lat_taps // 2, width, basis, channels)
    reach = lay.reach
    lat, lon = lax.axis_index("lat"), lax.axis_index("lon")
    even = lat % 2 == 0

    own = jnp.concatenate([features, cotangent], axis=0)
    west = shift(own, "lon", 1)
    own, lat_ext = lax.optimization_barrier((own, lat_ext))
    east = shift(own, "lon", -1)
    filters = make_filters(filter_taps, lat_ext, lon_count)
    filters = jnp.pad(jnp.swapaxes(filters, 1, 2), ((0, 0), (0, TAP_ROWS - lat_taps), (0, 0), (0, 0)))
    filters = filters.reshape(rows * TAP_ROWS, channels)

    late, filters = lax.optimization_barrier((own, filters))
    ahead = flip(late, "lat", 1)
    strip = jnp.concatenate([west, own, east], axis=1).reshape(2, rows, lay.strip, channels)
    message = jnp.concatenate([west.reshape(-1, channels), east.reshape(-1, channels), filters], axis=0)
    message, ahead = lax.optimization_barrier((message, ahead))
    sides = flip(message, "lat", 1)
    part = 2 * rows * width
    partner_taps = sides[2 * part :]
    partner = jnp.concatenate(
        [sides[:part].reshape(own.shape), ahead, sides[part : 2 * part].reshape(own.shape)], axis=1
    ).reshape(-1, channels)
    partner = jnp.concatenate([partner, partner_taps], axis=0)

    def edge(cells, taps, bottom):
        start = jnp.where(bottom, rows - reach, 0)
        cells = lax.dynamic_slice_in_dim(cells.reshape(strip.shape), start, reach, 1)
        taps = lax.dynamic_slice_in_dim(taps, start * TAP_ROWS, reach * TAP_ROWS, 0)
        return jnp.concatenate([cells.reshape(-1, channels), taps], axis=0)

    upper = (lat // 2) % 2 == 0
    beside = (lat % 2 == 1) == upper
    near = jnp.where(beside, edge(strip, filters, upper), edge(partner[: lay.cells], partner_taps, upper))
    at = (lat % 2) * rows * lay.strip + jnp.where(upper, rows - reach, 0) * lay.strip
    at_taps = jnp.where(upper, rows - reach, 0) * TAP_ROWS
    piece = jnp.where(
        beside,
        lax.dynamic_slice_in_dim(strip.reshape(-1, channels), at, lay.side, 0),
        lax.dynamic_slice_in_dim(partner, at, lay.side, 0),
    )
    piece_taps = jnp.where(
        beside,
        lax.dynamic_slice_in_dim(filters, at_taps, reach * TAP_ROWS, 0),
        lax.dynamic_slice_in_dim(partner_taps, at_taps, reach * TAP_ROWS, 0),
    )
    far = flip(jnp.concatenate([piece, piece_taps], axis=0), "lat", 2)

    def scratch(window_rows, basis_rows):
        return [
            pltpu.VMEM((2, window_rows, LANES, channels), jnp.bfloat16),
            pltpu.VMEM((window_rows, TAP_ROWS, channels), jnp.float32),
            pltpu.VMEM((basis_rows, channels), jnp.bfloat16),
        ]

    scale = 1.0 / math.sqrt(rows * lax.axis_size("lat") * width * lax.axis_size("lon"))
    share = jax.ShapeDtypeStruct((channels, channels), jnp.bfloat16)
    edges = scratch(2 * reach, 2 * lay.side)
    (grad,) = call(
        functools.partial(inner_kernel, lay, scale),
        [share],
        scratch(2 * rows, 2 * rows * lay.strip),
        INNER_FLOPS,
        "weight_inner",
    )(strip, filters, partner)
    outer = None
    if lax.axis_size("lat") > 4:
        bottom = jnp.logical_not(even)
        outward = edge(strip, filters, bottom)
        outer = outer_swap(outward, "lat")
        (grad,) = call(functools.partial(outer_kernel, lay, scale), [share], edges, MIDDLE_FLOPS, "weight_outer")(
            outward, outer, grad
        )
    got = flip(grad, "lat", 2)
    far, grad = lax.optimization_barrier((far, grad))
    passed = flip(far[: lay.side], "lat", 1)
    (middle,) = call(
        functools.partial(middle_kernel, lay, scale),
        [jax.ShapeDtypeStruct((channels, channels), jnp.float32)],
        edges,
        MIDDLE_FLOPS,
        "weight_middle",
    )(near, far, passed)
    grad = (grad.astype(jnp.float32) + got.astype(jnp.float32) + middle).astype(jnp.bfloat16)

    beyond = jnp.concatenate(
        [jnp.where(even, far[: lay.side], passed), jnp.where(even, passed, far[: lay.side]), far[lay.side :]], axis=0
    )
    outer = jnp.where(beside, beyond, jnp.zeros_like(beyond) if outer is None else outer)
    output, field_grad = call(
        functools.partial(field_kernel, lay),
        [jax.ShapeDtypeStruct(features.shape, jnp.bfloat16)] * 2,
        [
            pltpu.VMEM((2, rows + 2 * reach, LANES, channels), jnp.bfloat16),
            pltpu.VMEM((rows + 2 * reach, basis, TAP_ROWS, LANES), jnp.float32),
            pltpu.VMEM((basis, rows * width, channels), jnp.bfloat16),
        ],
        FIELD_FLOPS,
        "fields",
    )(
        strip,
        filters,
        partner,
        outer,
        filters[:, ::-1],
        edge(partner[: lay.cells], partner_taps, jnp.logical_not(even))[2 * lay.side :, ::-1],
        outer[2 * lay.side :, ::-1],
        weight,
    )

    lat_size, lon_size = lax.axis_size("lat"), lax.axis_size("lon")
    lat_bits = [1 << b for b in range(2, lat_size.bit_length() - 1)]
    lon_bits = [1 << b for b in range(1, lon_size.bit_length() - 1)]
    rounds = [(bit, bit, 0, 0) for bit in lat_bits]
    rounds += [(0, 0, up, down) for up, down in zip(lon_bits, lon_bits[::-1], strict=True)]
    for step, (lat_even, lat_odd, lon_even, lon_odd) in enumerate(rounds):
        if step == 1:
            grad, output, field_grad = lax.optimization_barrier((grad, output, field_grad))
        pairs = []
        for a in range(lat_size):
            lat_bit, lon_bit = (lat_odd, lon_odd) if a % 2 else (lat_even, lon_even)
            for o in range(lon_size):
                pairs.append((a * lon_size + o, (a ^ lat_bit) * lon_size + (o ^ lon_bit)))
        got = lax.ppermute(grad, ("lat", "lon"), pairs)
        grad = (grad.astype(jnp.float32) + got.astype(jnp.float32)).astype(jnp.bfloat16)
    got = flip(grad, "lon", 1)
    second = lon % 2 == 1
    grad = jnp.concatenate([jnp.where(second, got, grad), jnp.where(second, grad, got)], axis=0)
    got = flip(grad, "lat", 1)
    weight_grad = store(got, store(grad)).reshape(basis, channels, channels)
    return (output, field_grad, weight_grad)


def solution(mesh):
    in_specs = (
        P("lat", "lon", None),
        P("lat", "lon", None),
        P(),
        P("lat", None, None, None),
        P("lat"),
        P("lat"),
    )
    out_specs = (P("lat", "lon", None), P("lat", "lon", None), P())
    return jax.shard_map(
        per_device, mesh=mesh, in_specs=in_specs, out_specs=out_specs, check_vma=False
    )
```
